32 devices in a mesh: sub: 4 (over x, core), lat: 4 (over z), lon: 2 (over y).
Axes of the slice: x: 2, y: 2, z: 4, core: 2. Of those that a mesh axis runs over, the one named last changes fastest.
Arguments:
- increment: float32 [4, 64, 128, 512], P('sub', 'lat', 'lon'), may hold values from -6 to 6
- multiplier: float32 [4, 64, 128, 512], P('sub', 'lat', 'lon'), may hold values from -6 to 6
- background: bfloat16 [4, 64, 128, 512], P('sub', 'lat', 'lon'), may hold values from -6 to 6
- obs_cotangent: bfloat16 [4, 8, 2048, 512], P('sub', ('lat', 'lon')), may hold values from -6 to 6
- obs_column: int32 [4, 8, 2048], P('sub', ('lat', 'lon')), may hold values from 0 to 1023
- obs_count: int32 [4, 8], P('sub'), may hold values from 1 to 2048, 8192 in all within a row
- transport: float32 [8, 512], replicated, may hold values from 0.015 to 0.1
- hidden_weight: bfloat16 [512, 1024], replicated, may hold values from -0.25 to 0.25
- hidden_bias: float32 [1024], replicated, may hold values from -3 to 3
- output_weight: bfloat16 [1024, 512], replicated, may hold values from -0.1875 to 0.1875
Outputs:
- model_error: float32 [4, 64, 128, 512], P('sub', 'lat', 'lon')
- gradient: float32 [4, 64, 128, 512], P('sub', 'lat', 'lon')
- obs_tangent: bfloat16 [4, 8, 2048, 512], P('sub', ('lat', 'lon'))
The draws below stay inside these ranges and needn't reach their ends.
Inputs may be any that keep to these rules, and one draw needn't show every extreme that they name: `obs_count`: the counts of one subwindow sum to 8192, and one of them equals 2048. `obs_column`: slots at or beyond their block's count are unused.
All inputs are finite; a program needn't handle non-finite values.
Results may differ from the reference program's by a relative error of at most 0.0058.
Values may be sent and summed in bfloat16 or wider, within the bound.
A program may use at most 128 MiB of HBM per device.

```python
import math
import jax
import jax.numpy as jnp
import numpy as np
from jax import lax

LEV = 512
HID = 1024
CHAN = 512
LAT_DEV = 16
LON_DEV = 64
OBS_DEV = 2048
STEPS = 4
SUBS = 4
NLAT = 64
NLON = 128
OWNERS = 8
COLS = 1024
N_LAT = 4
N_LON = 2


def plant(entries, key, least, largest):
    spot = [jax.random.randint(jax.random.fold_in(key, axis), (), 0, length) for axis, length in enumerate(entries.shape)]
    main_axis = entries.shape.index(max(entries.shape))
    neighbour = spot[:main_axis] + [(spot[main_axis] + 1) % entries.shape[main_axis]] + spot[main_axis + 1:]
    return entries.at[tuple(spot)].set(least).at[tuple(neighbour)].set(largest)


def level_of(own_key, shape, pieces, low, high):
    def one(dim, parts):
        draws = jax.random.uniform(jax.random.fold_in(jax.random.fold_in(own_key, 6), dim), (parts,), jnp.float32, low / len(pieces), high / len(pieces))
        return jnp.repeat(jnp.exp(draws), shape[dim] // parts).reshape((-1,) + (1,) * (len(shape) - dim - 1))

    factor_of = one(*pieces[0])
    for cut in pieces[1:]:
        factor_of = factor_of * one(*cut)
    return factor_of


def profile(amount, total, limit, slope):
    weights = [(1 << 20) // math.isqrt(grade ** slope) + 1 for grade in range(2, amount + 1)]
    spare, counts = total - limit - (amount - 1), [1] * (amount - 1)
    while spare > 0:
        movable = [i for i in range(amount - 1) if counts[i] < limit]
        pool, budget = sum([weights[i] for i in movable]), spare
        for i in movable:
            extra = min(limit - counts[i], max(1, budget * weights[i] // pool), spare)
            counts[i] = counts[i] + extra
            spare = spare - extra
    return np.array([limit] + counts)


def ragged_sizes(key, number_of, total, most, slope):
    if number_of == 2:
        one = jax.random.randint(key, (), max(1, total - most), min(most, total - 1) + 1)
        return jnp.stack([one, total - one])
    tallies = jnp.asarray(profile(number_of, total, most, slope), jnp.int32)
    pairs = (number_of - 1) // 2
    donor, taker = tallies[1:1 + 2 * pairs:2], tallies[2:2 + 2 * pairs:2]
    margin = jnp.minimum(donor - 1, most - taker)
    passed = jax.random.randint(jax.random.fold_in(key, 1), (pairs,), 0, 1 << 20) % (margin + 1)
    tallies = tallies.at[1:1 + 2 * pairs:2].set(donor - passed).at[2:2 + 2 * pairs:2].set(taker + passed)
    return tallies[jax.random.permutation(jax.random.fold_in(key, 2), number_of)]


def noise(key, extent, scale, most, shards=(), kind=jnp.bfloat16):
    values = scale * jax.random.normal(key, extent, jnp.float32)
    if shards:
        values = values * level_of(key, extent, shards, -0.22, 0.18)
    return jnp.clip(values, -most, most).astype(kind)


def setup_inputs(seed: int = 0) -> dict:
    key_list = jax.random.split(jax.random.key(seed), 11)
    increment = noise(key_list[0], (SUBS, NLAT, NLON, LEV), 1.0, 6.0, ((0, 4), (1, 4), (2, 2)), jnp.float32)
    multiplier = noise(key_list[1], (SUBS, NLAT, NLON, LEV), 1.0, 6.0, ((0, 4), (1, 4), (2, 2)), jnp.float32)
    background = noise(key_list[2], (SUBS, NLAT, NLON, LEV), 1.0, 6.0, ((0, 4), (1, 4), (2, 2)))
    obs_cotangent = noise(key_list[3], (SUBS, OWNERS, OBS_DEV, CHAN), 1.0, 6.0, ((0, 4), (1, 8)))
    obs_column = plant(jax.random.randint(key_list[4], (SUBS, OWNERS, OBS_DEV), 0, COLS), jax.random.fold_in(key_list[4], 1), 0, COLS - 1).astype(jnp.int32)
    obs_count = jax.vmap(lambda own: ragged_sizes(own, OWNERS, OWNERS * OBS_DEV // 2, OBS_DEV, 2))(jax.random.split(key_list[5], SUBS)).reshape((SUBS, OWNERS)).astype(jnp.int32)
    transport = jnp.clip(jnp.exp(jax.random.uniform(key_list[6], (8, LEV), jnp.float32, math.log(0.015), math.log(0.1))), 0.015, 0.1)
    hidden_weight = noise(key_list[7], (LEV, HID), LEV ** -0.5, 0.25)
    hidden_bias = noise(key_list[8], (HID,), 0.5, 3.0, (), jnp.float32)
    output_weight = noise(key_list[9], (HID, CHAN), HID ** -0.5, 0.1875)
    return dict(increment=increment, multiplier=multiplier, background=background, obs_cotangent=obs_cotangent, obs_column=obs_column, obs_count=obs_count, transport=transport, hidden_weight=hidden_weight, hidden_bias=hidden_bias, output_weight=output_weight)


def observe(state_rows, back_rows, cot_rows, hidden_weight, hidden_bias, output_weight):
    preact = jnp.dot(back_rows, hidden_weight, preferred_element_type=jnp.float32) + hidden_bias
    hidden = jnp.tanh(preact)
    slopes = 1.0 - hidden * hidden
    forward = jnp.dot(state_rows, hidden_weight, preferred_element_type=jnp.float32)
    scaled = (slopes * forward).astype(jnp.bfloat16)
    tangent = jnp.dot(scaled, output_weight, preferred_element_type=jnp.float32).astype(jnp.bfloat16)
    pulled = jnp.dot(cot_rows, output_weight.T, preferred_element_type=jnp.float32)
    weighted = (slopes * pulled).astype(jnp.bfloat16)
    adjoint = jnp.dot(weighted, hidden_weight.T, preferred_element_type=jnp.float32).astype(jnp.bfloat16)
    return tangent, adjoint


def mirrored(transport):
    return jnp.stack([transport[3], transport[2], transport[1], transport[0],
                      transport[7], transport[6], transport[5], transport[4]])


def advance(window, coeffs):
    total_rate = jnp.sum(coeffs, axis=0)
    height = window.shape[0]
    across = window.shape[1]
    for sweep_step in range(STEPS):
        padded = jnp.pad(window, ((2, 2), (2, 2), (0, 0)))
        window = ((1.0 - total_rate) * window
                  + coeffs[0] * padded[0:height, 2:across + 2]
                  + coeffs[1] * padded[1:height + 1, 2:across + 2]
                  + coeffs[2] * padded[3:height + 3, 2:across + 2]
                  + coeffs[3] * padded[4:height + 4, 2:across + 2]
                  + coeffs[4] * padded[2:height + 2, 0:across]
                  + coeffs[5] * padded[2:height + 2, 1:across + 1]
                  + coeffs[6] * padded[2:height + 2, 3:across + 3]
                  + coeffs[7] * padded[2:height + 2, 4:across + 4])
    return window


def to_blocks(full_field):
    shaped = full_field.reshape(SUBS, N_LAT, LAT_DEV, N_LON, LON_DEV, full_field.shape[-1])
    return shaped.transpose(0, 1, 3, 2, 4, 5).reshape(SUBS * OWNERS, COLS, full_field.shape[-1])


def reference(increment, multiplier, background, obs_cotangent, obs_column, obs_count, transport, hidden_weight, hidden_bias, output_weight):
    reverse_rates = mirrored(transport)
    ahead = lax.map(lambda window: advance(window, transport), increment)
    behind = lax.map(lambda window: advance(window, reverse_rates), multiplier)
    zero_slab = jnp.zeros_like(increment[0:1])
    model_error = increment - jnp.concatenate([zero_slab, ahead[:-1]], axis=0)
    state_blocks = to_blocks(increment)
    back_blocks = to_blocks(background)
    flat_columns = obs_column.reshape(SUBS * OWNERS, OBS_DEV)
    flat_cot = obs_cotangent.reshape(SUBS * OWNERS, OBS_DEV, CHAN)
    flat_count = obs_count.reshape(SUBS * OWNERS)

    def one_block(inputs):
        state_block, back_block, columns, cot_rows, slot_count = inputs
        alive_rows = (jnp.arange(OBS_DEV, dtype=jnp.int32) < slot_count)[:, None]
        tangent, adjoint = observe(state_block[columns].astype(jnp.bfloat16), back_block[columns], cot_rows,
                                   hidden_weight, hidden_bias, output_weight)
        tangent = jnp.where(alive_rows, tangent, jnp.zeros_like(tangent))
        adjoint_wide = jnp.where(alive_rows, adjoint.astype(jnp.float32), jnp.zeros((), jnp.float32))
        summed = jnp.zeros((COLS, LEV), jnp.float32).at[columns].add(adjoint_wide)
        return tangent, summed

    tangents, sums = lax.map(one_block, (state_blocks, back_blocks, flat_columns, flat_cot, flat_count))
    obs_tangent = tangents.reshape(SUBS, OWNERS, OBS_DEV, CHAN)
    obs_adjoint = sums.reshape(SUBS, N_LAT, N_LON, LAT_DEV, LON_DEV, LEV).transpose(0, 1, 3, 2, 4, 5).reshape(SUBS, NLAT, NLON, LEV)
    gradient = multiplier - jnp.concatenate([behind[1:], zero_slab], axis=0) + obs_adjoint
    return model_error, gradient, obs_tangent
```

```python
import functools

import jax
import jax.numpy as jnp
from jax import lax
from jax.experimental import pallas as pl
from jax.experimental.pallas import tpu as pltpu
from jax.sharding import PartitionSpec as P

STEPS = 4
REACH = 2
HALO = STEPS * REACH
SUB = 8
LANES = 128
NT = (((1,), (1,)), ((), ()))
F32 = jnp.float32
BF16 = jnp.bfloat16


def dot(a, b):
    return jnp.dot(a, b, preferred_element_type=F32)


def dot_nt(a, b):
    return lax.dot_general(a, b, NT, preferred_element_type=F32)


def observe_kernel(count_ref, cols_ref, state_ref, back_ref, cot_ref, hw_ref, bias_ref, ow_ref,
                   tangent_ref, adjoint_ref, per_column, slot_cols):
    columns, levels = state_ref.shape
    slots = cot_ref.shape[0]
    count = count_ref[0]
    tile = min(256, columns)
    chunks = slots // LANES
    place = (lax.broadcasted_iota(jnp.int32, (chunks, LANES), 0) * LANES
             + lax.broadcasted_iota(jnp.int32, (chunks, LANES), 1))
    slot_cols[...] = jnp.where(place < count, cols_ref[...], -1)

    @pl.loop(0, columns // tile)
    def _(t):
        base = pl.multiple_of(t * tile, tile)
        rows = pl.ds(base, tile)
        wanted = lax.broadcasted_iota(jnp.int32, (tile, LANES), 0) + base
        hits = [jnp.where(slot_cols[k:k + 1, :] == wanted, 1.0, 0.0).astype(BF16) for k in range(chunks)]
        summed = dot(jnp.concatenate(hits, axis=1), cot_ref[...]).astype(BF16)
        hidden = jnp.tanh(dot(back_ref[rows, :], hw_ref[...]) + bias_ref[...])
        slopes = 1.0 - hidden * hidden
        forward = dot(state_ref[rows, :].astype(BF16), hw_ref[...])
        per_column[rows, :] = dot((slopes * forward).astype(BF16), ow_ref[...]).astype(BF16)
        pulled = dot_nt(summed, ow_ref[...])
        adjoint_ref[rows, :] = dot_nt((slopes * pulled).astype(BF16), hw_ref[...])

    @pl.loop(0, slots // 256)
    def _(t):
        parts = []
        for h in range(2):
            named = jnp.transpose(jnp.broadcast_to(slot_cols[pl.ds(t * 2 + h, 1), :], (LANES, LANES)))
            lane = lax.broadcasted_iota(jnp.int32, (LANES, LANES), 1)
            hits = [jnp.where(named == lane + c * LANES, 1.0, 0.0).astype(BF16) for c in range(columns // LANES)]
            parts.append(jnp.concatenate(hits, axis=1))
        tangent_ref[pl.ds(pl.multiple_of(t * 256, 256), 256), :] = dot(
            jnp.concatenate(parts, axis=0), per_column[...]).astype(BF16)


def observe(count, cols, state, back, cot, hw, bias, ow):
    columns, levels = state.shape
    slots, chan = cot.shape
    hid = hw.shape[1]
    vm = pl.BlockSpec(memory_space=pltpu.VMEM)
    flops = 2 * columns * levels * hid * 5 + 4 * columns * slots * chan
    return pl.pallas_call(
        observe_kernel,
        out_shape=(jax.ShapeDtypeStruct((slots, chan), BF16), jax.ShapeDtypeStruct((columns, levels), F32)),
        in_specs=[pl.BlockSpec(memory_space=pltpu.SMEM)] + [vm] * 7,
        out_specs=(vm, vm),
        scratch_shapes=[pltpu.VMEM((columns, chan), BF16), pltpu.VMEM((slots // LANES, LANES), jnp.int32)],
        compiler_params=pltpu.CompilerParams(vmem_limit_bytes=40 << 20),
        cost_estimate=pl.CostEstimate(flops=flops, bytes_accessed=14 << 20, transcendentals=columns * hid),
        name="observe",
    )(count, cols, state, back, cot, hw, bias, ow)


def transport_field(lat_first, lat_last, lon_first, center, above, below, side, weights, window, state, width, n_lon):
    height = center.shape[0]
    across = center.shape[1]
    total = height + 2 * HALO
    start = jnp.where(lon_first, 0, HALO) if n_lon > 1 else 0
    side_at = jnp.where(lon_first, across, 0)
    if n_lon > 1:
        start = pl.multiple_of(start, HALO)
        side_at = pl.multiple_of(side_at, HALO)
    window[pl.ds(0, HALO), pl.ds(start, across), :] = above[...].astype(F32)
    window[pl.ds(HALO, height), pl.ds(start, across), :] = center[...].astype(F32)
    window[pl.ds(HALO + height, HALO), pl.ds(start, across), :] = below[...].astype(F32)
    if n_lon > 1:
        window[:, pl.ds(side_at, HALO), :] = side[...].astype(F32)

    @pl.loop(0, total)
    def _(r):
        for v in range(width):
            state[0, r, v] = window[r, pl.ds(v, SUB, stride=width), :]

    @pl.when(jnp.logical_or(lat_first, lat_last))
    def _():
        zero = jnp.zeros((HALO, width, SUB, LANES), F32)

        @pl.when(lat_first)
        def _():
            state[1, pl.ds(0, HALO)] = zero

        @pl.when(lat_last)
        def _():
            state[1, pl.ds(HALO + height, HALO)] = zero

    lane_row = lax.broadcasted_iota(jnp.int32, (SUB, LANES), 0)
    low_edge = lane_row == 0
    high_edge = lane_row == SUB - 1
    c = [jnp.broadcast_to(weights[k:k + 1, :], (SUB, LANES)) for k in range(9)]
    for step in range(STEPS):
        src, dst = step % 2, (step + 1) % 2
        lo = REACH * (step + 1)
        first = jnp.where(lat_first, HALO, lo)
        last = jnp.where(lat_last, HALO + height, total - lo)

        @pl.loop(first, last)
        def _(r):
            row = [state[src, r, v] for v in range(width)]
            before = [jnp.where(low_edge, 0.0, pltpu.roll(row[width - REACH + k], 1, 0)) for k in range(REACH)]
            after = [jnp.where(high_edge, 0.0, pltpu.roll(row[k], SUB - 1, 0)) for k in range(REACH)]
            line = before + row + after
            for v in range(width):
                acc = c[8] * row[v]
                acc += c[0] * state[src, r - 2, v]
                acc += c[1] * state[src, r - 1, v]
                acc += c[2] * state[src, r + 1, v]
                acc += c[3] * state[src, r + 2, v]
                acc += c[4] * line[v]
                acc += c[5] * line[v + 1]
                acc += c[6] * line[v + 3]
                acc += c[7] * line[v + 4]
                if step == STEPS - 1:
                    window[r, pl.ds(v, SUB, stride=width), :] = acc
                else:
                    state[dst, r, v] = acc
    return start


def transport_kernel(axes, width, wa_ref, wm_ref, a_mid, a_up, a_down, a_side, m_mid, m_up, m_down, m_side,
                     inc_ref, mul_ref, adj_ref, err_ref, grad_ref, window, state):
    n_lat, n_lon = axes
    lat = lax.axis_index("lat")
    lon = lax.axis_index("lon")
    height, across = a_mid.shape[0], a_mid.shape[1]
    place = (lat == 0, lat == n_lat - 1, lon == 0)
    start = transport_field(*place, a_mid, a_up, a_down, a_side, wa_ref, window, state, width, n_lon)
    err_ref[...] = inc_ref[...] - window[pl.ds(HALO, height), pl.ds(start, across), :]
    start = transport_field(*place, m_mid, m_up, m_down, m_side, wm_ref, window, state, width, n_lon)
    grad_ref[...] = mul_ref[...] - window[pl.ds(HALO, height), pl.ds(start, across), :] + adj_ref[...]


def transport_call(axes, wa, wm, a_parts, m_parts, inc, mul, adj):
    n_lat, n_lon = axes
    height, across, levels = inc.shape
    width = (across + (HALO if n_lon > 1 else 0)) // SUB
    total = height + 2 * HALO
    whole = lambda rows, cols: pl.BlockSpec((rows, cols, LANES), lambda g: (0, 0, g))
    field = [whole(height, across), whole(HALO, across), whole(HALO, across), whole(total, HALO)]
    w_spec = pl.BlockSpec((9, LANES), lambda g: (0, g))
    return pl.pallas_call(
        functools.partial(transport_kernel, axes, width),
        grid=(levels // LANES,),
        out_shape=(jax.ShapeDtypeStruct(inc.shape, F32),) * 2,
        in_specs=[w_spec, w_spec] + field + field + [whole(height, across)] * 3,
        out_specs=(whole(height, across),) * 2,
        scratch_shapes=[
            pltpu.VMEM((total, width * SUB, LANES), F32),
            pltpu.VMEM((2, total, width, SUB, LANES), F32),
        ],
        compiler_params=pltpu.CompilerParams(vmem_limit_bytes=40 << 20),
        cost_estimate=pl.CostEstimate(flops=2 * 4 * 17 * height * across * levels, bytes_accessed=18 << 20, transcendentals=0),
        name="transport",
    )(wa, wm, *a_parts, *m_parts, inc, mul, adj)


def shifted(array, axis, by):
    count = lax.axis_size(axis)
    pairs = [(i, i + by) for i in range(count) if 0 <= i + by < count]
    return lax.ppermute(array, axis, pairs)


def with_halo(mid):
    height, across, levels = mid.shape
    up = shifted(mid[height - HALO:], "lat", 1)
    down = shifted(mid[:HALO], "lat", -1)
    if lax.axis_size("lon") == 1:
        return mid, up, down, jnp.zeros((height + 2 * HALO, HALO, levels), mid.dtype)
    first = lax.axis_index("lon") == 0
    edge = lambda x: lax.dynamic_slice_in_dim(x, jnp.where(first, across - HALO, 0), HALO, axis=1)
    side = lax.ppermute(jnp.concatenate([edge(up), edge(mid), edge(down)], axis=0), "lon", [(0, 1), (1, 0)])
    return mid, up, down, side


def local(increment, multiplier, background, obs_cotangent, obs_column, obs_count, transport,
          hidden_weight, hidden_bias, output_weight):
    n_lat, n_lon = lax.axis_size("lat"), lax.axis_size("lon")
    assert n_lon <= 2
    inc, mul = increment[0], multiplier[0]
    levels = inc.shape[-1]
    rest = (1.0 - jnp.sum(transport, axis=0))[None]
    wa = jnp.concatenate([transport, rest], axis=0)
    wm = jnp.concatenate([transport[3::-1], transport[7:3:-1], rest], axis=0)
    a_parts = with_halo(shifted(inc.astype(BF16), "sub", 1))
    m_parts = with_halo(shifted(mul.astype(BF16), "sub", -1))
    myself = lax.axis_index(("lat", "lon"))
    count = lax.dynamic_slice_in_dim(obs_count[0], myself, 1)
    tangent, adj = observe(count, obs_column.reshape(-1, LANES), inc.reshape(-1, levels),
                           background.reshape(-1, levels), obs_cotangent[0, 0], hidden_weight,
                           hidden_bias[None], output_weight)
    err, grad = transport_call((n_lat, n_lon), wa, wm, a_parts, m_parts, inc, mul, adj.reshape(inc.shape))
    return err[None], grad[None], tangent[None, None]


def solution(mesh):
    field = P("sub", "lat", "lon", None)
    slots = P("sub", ("lat", "lon"), None, None)
    in_specs = (field, field, field, slots, P("sub", ("lat", "lon"), None), P("sub", None), P(), P(), P(), P())
    return jax.shard_map(local, mesh=mesh, in_specs=in_specs, out_specs=(field, field, slots), check_vma=False)
```

```python
import functools

import jax
import jax.numpy as jnp
from jax import lax
from jax.experimental import pallas as pl
from jax.experimental.pallas import tpu as pltpu
from jax.sharding import PartitionSpec as P

STEPS = 4
REACH = 2
HALO = STEPS * REACH
SUB = 8
LANES = 128
BLOCK = 4
MESH = pl.DeviceIdType.MESH
NT = (((1,), (1,)), ((), ()))
F32 = jnp.float32
BF16 = jnp.bfloat16


def dot(a, b):
    return jnp.dot(a, b, preferred_element_type=F32)


def dot_nt(a, b):
    return lax.dot_general(a, b, NT, preferred_element_type=F32)


CENTER, UP, DOWN, SIDE = 0, 2, 3, 4
KINDS = 7


def exchange_kernel(sizes, count_ref, cols_hbm, inc_hbm, mul_hbm, back_hbm, cot_hbm, hw_hbm, bias_hbm, ow_hbm,
                    field_out, side_out, tangent_out, adjoint_out,
                    cols, raw, sent, back, cot, hw, bias, ow, field, side, stage,
                    per_column, slot_cols, tangent, adjoint,
                    load_sem, send_sem, recv_sem, out_sem, tan_sem, adj_sem):
    n_sub, n_lat, n_lon = sizes
    sub, lat, lon = lax.axis_index("sub"), lax.axis_index("lat"), lax.axis_index("lon")
    height, across, levels = inc_hbm.shape
    columns = height * across
    slots = cot.shape[0]
    odd = sub % 2
    near, far = sub + 1 - 2 * odd, sub - 1 + 2 * odd
    has_near = near < n_sub
    has_far = jnp.logical_and(far >= 0, far < n_sub)
    near_field, far_field = 1 - odd, odd
    has_above, has_below = lat > 0, lat < n_lat - 1

    loads = [(inc_hbm, raw.at[0]), (mul_hbm, raw.at[1]), (cols_hbm, cols), (cot_hbm, cot), (back_hbm, back),
             (hw_hbm, hw), (bias_hbm, bias), (ow_hbm, ow)]
    loads = [pltpu.make_async_copy(a, b, load_sem.at[k]) for k, (a, b) in enumerate(loads)]
    for load in loads:
        load.start()

    barrier = pltpu.get_barrier_semaphore()
    others = [({"sub": near}, has_near), ({"sub": far}, has_far), ({"lat": lat - 1}, has_above), ({"lat": lat + 1}, has_below)]
    amount = sum(have.astype(jnp.int32) for _, have in others)
    for target, have in others:
        @pl.when(have)
        def _(target=target):
            pl.semaphore_signal(barrier, inc=1, device_id=target, device_id_type=MESH)
    if n_lon > 1:
        pl.semaphore_signal(barrier, inc=1, device_id={"lon": 1 - lon}, device_id_type=MESH)
        amount = amount + 1

    def copy(f, kind, src, dst, target):
        return pltpu.make_async_remote_copy(src_ref=src, dst_ref=dst, send_sem=send_sem.at[f, kind],
                                            recv_sem=recv_sem.at[f, kind], device_id=target, device_id_type=MESH)

    def center(f, part, target):
        return copy(f, CENTER + part, sent.at[f, pl.ds(part * HALO, HALO)],
                    field.at[f, pl.ds(HALO + part * HALO, HALO)], target)

    def upward(f):
        return copy(f, DOWN, field.at[f, pl.ds(HALO, HALO)], field.at[f, pl.ds(HALO + height, HALO)], {"lat": lat - 1})

    def downward(f):
        return copy(f, UP, field.at[f, pl.ds(height, HALO)], field.at[f, pl.ds(0, HALO)], {"lat": lat + 1})

    def sideways(f, k):
        lo, amount = ((HALO // 2, height // 2), (0, HALO // 2), ((HALO + height) // 2, HALO // 2))[k]
        return copy(f, SIDE + k, stage.at[f, pl.ds(lo, amount)], side.at[f, pl.ds(lo, amount)], {"lon": 1 - lon})

    def keep(f, k):
        lo, amount = ((HALO, height), (0, HALO), (HALO + height, HALO))[k]
        rows = pl.ds(lo, amount)
        return pltpu.make_async_copy(field.at[f, rows], field_out.at[f, rows], out_sem.at[f, k])

    def pass_on(f, k):
        keep(f, k).start()
        if n_lon > 1:
            lo, amount = ((HALO // 2, height // 2), (0, HALO // 2), ((HALO + height) // 2, HALO // 2))[k]

            @pl.loop(lo, lo + amount)
            def _(p):
                pair = []
                for q in range(2):
                    row = field[f, 2 * p + q].astype(F32)
                    pair.append(jnp.where(lon == 0, row[across - HALO:], row[:HALO]))
                stage[f, p] = jnp.concatenate(pair, axis=0).astype(BF16)
            sideways(f, k).start()

    def take_center(f, source):
        center(f, 0, {"sub": source}).wait_recv()

        @pl.when(has_above)
        def _():
            upward(f).start()
        center(f, 1, {"sub": source}).wait_recv()

        @pl.when(has_below)
        def _():
            downward(f).start()
        pass_on(f, 0)

    def take_halo(f):
        @pl.when(has_above)
        def _():
            downward(f).wait_recv()
            pass_on(f, 1)

        @pl.when(has_below)
        def _():
            upward(f).wait_recv()
            pass_on(f, 2)

    def finish(f):
        def close(k):
            keep(f, k).wait()
            if n_lon > 1:
                sideways(f, k).wait()
        close(0)

        @pl.when(has_above)
        def _():
            upward(f).wait_send()
            close(1)

        @pl.when(has_below)
        def _():
            downward(f).wait_send()
            close(2)

    loads[0].wait()
    sent[0] = raw[0].astype(BF16)
    loads[1].wait()
    sent[1] = raw[1].astype(BF16)
    pl.semaphore_wait(barrier, amount)

    @pl.when(has_far)
    def _():
        for part in range(2):
            center(near_field, part, {"sub": far}).start()

    @pl.when(has_near)
    def _():
        for part in range(2):
            center(far_field, part, {"sub": near}).start()

    for load in loads[2:]:
        load.wait()
    count = count_ref[0]
    tile = 256
    chunks = slots // LANES
    place = (lax.broadcasted_iota(jnp.int32, (chunks, LANES), 0) * LANES
             + lax.broadcasted_iota(jnp.int32, (chunks, LANES), 1))
    slot_cols[...] = jnp.where(place < count, cols[...], -1)

    def adjoint_copy(t):
        rows = pl.ds(pl.multiple_of(t * tile, tile), tile)
        return pltpu.make_async_copy(adjoint.at[rows], adjoint_out.at[rows], adj_sem.at[t])

    def tangent_copy(t):
        rows = pl.ds(pl.multiple_of(t * tile, tile), tile)
        return pltpu.make_async_copy(tangent.at[rows], tangent_out.at[rows], tan_sem.at[t])

    def observe_columns(t):
        base = pl.multiple_of(t * tile, tile)
        rows = pl.ds(base, tile)
        wanted = lax.broadcasted_iota(jnp.int32, (tile, LANES), 0) + base
        hits = [jnp.where(slot_cols[k:k + 1, :] == wanted, 1.0, 0.0).astype(BF16) for k in range(chunks)]
        summed = dot(jnp.concatenate(hits, axis=1), cot[...]).astype(BF16)
        hidden = jnp.tanh(dot(back[rows, :], hw[...]) + bias[...])
        slopes = 1.0 - hidden * hidden
        state = sent[0, pl.ds(t * (tile // across), tile // across)].reshape(tile, levels)
        forward = dot(state, hw[...])
        per_column[rows, :] = dot((slopes * forward).astype(BF16), ow[...]).astype(BF16)
        pulled = dot_nt(summed, ow[...])
        adjoint[rows, :] = dot_nt((slopes * pulled).astype(BF16), hw[...])
        adjoint_copy(t).start()

    def observe_slots(t):
        parts = []
        for h in range(tile // LANES):
            named = jnp.transpose(jnp.broadcast_to(slot_cols[pl.ds(t * (tile // LANES) + h, 1), :], (LANES, LANES)))
            lane = lax.broadcasted_iota(jnp.int32, (LANES, LANES), 1)
            hits = [jnp.where(named == lane + c * LANES, 1.0, 0.0).astype(BF16) for c in range(columns // LANES)]
            parts.append(jnp.concatenate(hits, axis=1))
        tangent[pl.ds(pl.multiple_of(t * tile, tile), tile), :] = dot(
            jnp.concatenate(parts, axis=0), per_column[...]).astype(BF16)
        tangent_copy(t).start()

    column_tiles, slot_tiles = columns // tile, slots // tile
    pl.loop(0, 1)(observe_columns)

    @pl.when(has_near)
    def _():
        take_center(near_field, near)
    pl.loop(1, column_tiles)(observe_columns)

    @pl.when(has_far)
    def _():
        take_center(far_field, far)
    pl.loop(0, slot_tiles // 2)(observe_slots)

    @pl.when(has_near)
    def _():
        take_halo(near_field)
    pl.loop(slot_tiles // 2, slot_tiles)(observe_slots)

    @pl.when(has_far)
    def _():
        take_halo(far_field)

    for have, f, source in ((has_near, near_field, near), (has_far, far_field, far)):
        @pl.when(have)
        def _(f=f, source=source):
            finish(f)
            for part in range(2):
                center(1 - f, part, {"sub": source}).wait_send()

    if n_lon > 1:
        kept = pltpu.make_async_copy(side, side_out, load_sem.at[0])
        kept.start()
        kept.wait()
    for t in range(column_tiles):
        adjoint_copy(t).wait()
    for t in range(slot_tiles):
        tangent_copy(t).wait()


def exchange(sizes, count, cols, inc, mul, back, cot, hw, bias, ow):
    height, across, levels = inc.shape
    columns = height * across
    slots, chan = cot.shape
    hid = hw.shape[1]
    total = height + 2 * HALO
    anywhere = pl.BlockSpec(memory_space=pl.ANY)
    vm = pltpu.VMEM
    dma = pltpu.SemaphoreType.DMA
    field_shape, side_shape = (2, total, across, levels), (2, total // 2, 2 * HALO, levels)
    flops = 2 * columns * levels * hid * 5 + 4 * columns * slots * chan
    return pl.pallas_call(
        functools.partial(exchange_kernel, sizes),
        out_shape=(jax.ShapeDtypeStruct(field_shape, BF16), jax.ShapeDtypeStruct(side_shape, BF16),
                   jax.ShapeDtypeStruct((slots, chan), BF16), jax.ShapeDtypeStruct((columns, levels), F32)),
        in_specs=[pl.BlockSpec(memory_space=pltpu.SMEM)] + [anywhere] * 8,
        out_specs=(anywhere,) * 4,
        scratch_shapes=[
            vm(cols.shape, jnp.int32), vm((2,) + inc.shape, F32), vm((2,) + inc.shape, BF16),
            vm(back.shape, BF16), vm(cot.shape, BF16), vm(hw.shape, BF16), vm(bias.shape, F32), vm(ow.shape, BF16),
            vm(field_shape, BF16), vm(side_shape, BF16), vm(side_shape, BF16),
            vm((columns, chan), BF16), vm(cols.shape, jnp.int32), vm((slots, chan), BF16), vm((columns, levels), F32),
            dma((8,)), dma((2, KINDS)), dma((2, KINDS)), dma((2, 3)), dma((slots // 256,)), dma((columns // 256,)),
        ],
        compiler_params=pltpu.CompilerParams(vmem_limit_bytes=52 << 20, collective_id=0, has_side_effects=True),
        cost_estimate=pl.CostEstimate(flops=flops, bytes_accessed=20 << 20, transcendentals=columns * hid),
        name="exchange",
    )(count, cols, inc, mul, back, cot, hw, bias, ow)


def transport_field(lat_first, lat_last, start, side_at, field, side, f, weights, window, one, two, width, n_lon):
    total, across = field.shape[1], field.shape[2]
    window[:, pl.ds(start, across), :] = field[f].astype(F32)
    if n_lon > 1:
        for p in range(total // 2):
            pair = side[f, p].astype(F32)
            window[2 * p, pl.ds(side_at, HALO), :] = pair[:HALO]
            window[2 * p + 1, pl.ds(side_at, HALO), :] = pair[HALO:]

    lane_row = lax.broadcasted_iota(jnp.int32, (SUB, LANES), 0)
    low_edge = lane_row == 0
    high_edge = lane_row == SUB - 1

    def put(ref, r, v, vec):
        ref[r, v + REACH] = vec
        if v >= width - REACH:
            ref[r, v - (width - REACH)] = jnp.where(low_edge, 0.0, pltpu.roll(vec, 1, 0))
        if v < REACH:
            ref[r, v + width + REACH] = jnp.where(high_edge, 0.0, pltpu.roll(vec, SUB - 1, 0))

    def clear_outside(ref):
        zero = jnp.zeros((HALO,) + ref.shape[1:], F32)

        @pl.when(lat_first)
        def _():
            ref[pl.ds(0, HALO)] = zero

        @pl.when(lat_last)
        def _():
            ref[pl.ds(total - HALO, HALO)] = zero

    @pl.loop(0, total // 2)
    def _(p):
        for q in range(2):
            for v in range(width):
                put(one, 2 * p + q, v, window[2 * p + q, pl.ds(v, SUB, stride=width), :])
    clear_outside(one)

    c = [jnp.broadcast_to(weights[k:k + 1, :], (SUB, LANES)) for k in range(9)]
    for step in range(STEPS):
        src, dst = (one, two) if step % 2 == 0 else (two, one)
        lo = REACH * (step + 1)

        @pl.loop(0, (total - 2 * lo) // BLOCK)
        def _(b):
            r = lo + b * BLOCK
            for v in range(width):
                tall = [src[r + k - REACH, v + REACH] for k in range(BLOCK + 2 * REACH)]
                for q in range(BLOCK):
                    line = [src[r + q, v + k] for k in (0, 1, 3, 4)]
                    acc = ((c[8] * tall[q + 2] + c[0] * tall[q]) + (c[1] * tall[q + 1] + c[2] * tall[q + 3])
                           + (c[3] * tall[q + 4] + c[5] * line[1])
                           + ((c[4] * line[0] + c[6] * line[2]) + c[7] * line[3]))
                    if step == STEPS - 1:
                        window[r + q, pl.ds(v, SUB, stride=width), :] = acc
                    else:
                        put(dst, r + q, v, acc)
        if step < STEPS - 1:
            clear_outside(dst)


def transport_kernel(sizes, width, wa_ref, wm_ref, field, side, inc_ref, mul_ref, adj_ref, err_ref, grad_ref,
                     window, one, two):
    n_sub, n_lat, n_lon = sizes
    sub, lat, lon = lax.axis_index("sub"), lax.axis_index("lat"), lax.axis_index("lon")
    height, across = inc_ref.shape[0], inc_ref.shape[1]
    start = pl.multiple_of(jnp.where(lon == 0, 0, HALO), HALO) if n_lon > 1 else 0
    side_at = pl.multiple_of(jnp.where(lon == 0, across, 0), HALO)
    place = (lat == 0, lat == n_lat - 1, start, side_at, field, side)
    rest = (window, one, two, width, n_lon)
    result = (pl.ds(HALO, height), pl.ds(start, across))

    @pl.when(sub > 0)
    def _():
        transport_field(*place, 0, wa_ref, *rest)
        err_ref[...] = inc_ref[...] - window[result]

    @pl.when(sub == 0)
    def _():
        err_ref[...] = inc_ref[...]

    @pl.when(sub < n_sub - 1)
    def _():
        transport_field(*place, 1, wm_ref, *rest)
        grad_ref[...] = mul_ref[...] - window[result] + adj_ref[...]

    @pl.when(sub == n_sub - 1)
    def _():
        grad_ref[...] = mul_ref[...] + adj_ref[...]


def transport_call(sizes, wa, wm, field, side, inc, mul, adj):
    height, across, levels = inc.shape
    width = (across + (HALO if sizes[2] > 1 else 0)) // SUB
    total = height + 2 * HALO
    def whole(shape):
        return pl.BlockSpec(shape[:-1] + (LANES,), lambda g: (0,) * (len(shape) - 1) + (g,))
    arrays = (wa, wm, field, side, inc, mul, adj)
    state = pltpu.VMEM((total, width + 2 * REACH, SUB, LANES), F32)
    return pl.pallas_call(
        functools.partial(transport_kernel, sizes, width),
        grid=(levels // LANES,),
        out_shape=(jax.ShapeDtypeStruct(inc.shape, F32),) * 2,
        in_specs=[whole(x.shape) for x in arrays],
        out_specs=(whole(inc.shape),) * 2,
        scratch_shapes=[pltpu.VMEM((total, width * SUB, LANES), F32), state, state],
        compiler_params=pltpu.CompilerParams(vmem_limit_bytes=40 << 20),
        cost_estimate=pl.CostEstimate(flops=2 * 4 * 17 * height * across * levels, bytes_accessed=18 << 20, transcendentals=0),
        name="transport",
    )(*arrays)


def local(increment, multiplier, background, obs_cotangent, obs_column, obs_count, transport,
          hidden_weight, hidden_bias, output_weight):
    sizes = tuple(lax.axis_size(name) for name in ("sub", "lat", "lon"))
    assert sizes[2] <= 2
    inc, mul = increment[0], multiplier[0]
    levels = inc.shape[-1]
    rest = (1.0 - jnp.sum(transport, axis=0))[None]
    wa = jnp.concatenate([transport, rest], axis=0)
    wm = jnp.concatenate([transport[3::-1], transport[7:3:-1], rest], axis=0)
    myself = lax.axis_index(("lat", "lon"))
    count = lax.dynamic_slice_in_dim(obs_count[0], myself, 1)
    field, side, tangent, adj = exchange(
        sizes, count, obs_column.reshape(-1, LANES), inc, mul, background.reshape(-1, levels), obs_cotangent[0, 0],
        hidden_weight, hidden_bias[None], output_weight)
    err, grad = transport_call(sizes, wa, wm, field, side, inc, mul, adj.reshape(inc.shape))
    return err[None], grad[None], tangent[None, None]


def solution(mesh):
    field = P("sub", "lat", "lon", None)
    slots = P("sub", ("lat", "lon"), None, None)
    in_specs = (field, field, field, slots, P("sub", ("lat", "lon"), None), P("sub", None), P(), P(), P(), P())
    return jax.shard_map(local, mesh=mesh, in_specs=in_specs, out_specs=(field, field, slots), check_vma=False)
```

```python
import functools

import jax
import jax.numpy as jnp
from jax import lax
from jax.experimental import pallas as pl
from jax.experimental.pallas import tpu as pltpu
from jax.sharding import PartitionSpec as P

STEPS = 4
REACH = 2
HALO = STEPS * REACH
SUB = 8
LANES = 128
BLOCK = 4
MESH = pl.DeviceIdType.MESH
NT = (((1,), (1,)), ((), ()))
F32 = jnp.float32
BF16 = jnp.bfloat16


def dot(a, b):
    return jnp.dot(a, b, preferred_element_type=F32)


def dot_nt(a, b):
    return lax.dot_general(a, b, NT, preferred_element_type=F32)


CENTER, UP, DOWN, SIDE = 0, 2, 3, 4
DIRECT = 7
KINDS = 9
VMEM_BYTES = 58 << 20


def exchange_kernel(sizes, count_ref, cols_hbm, inc_hbm, mul_hbm, back_hbm, cot_hbm, hw_hbm, bias_hbm, ow_hbm, rates_hbm,
                    field_out, side_out, tangent_out, adjoint_out, moved_out,
                    rates, moved, window, one, two, cols, raw, sent, back, cot, hw, bias, ow, field, side, stage,
                    per_column, slot_cols, tangent, adjoint,
                    load_sem, send_sem, recv_sem, out_sem, tan_sem, adj_sem, moved_sem):
    n_sub, n_lat, n_lon = sizes
    sub, lat, lon = lax.axis_index("sub"), lax.axis_index("lat"), lax.axis_index("lon")
    height, across, levels = inc_hbm.shape
    columns = height * across
    slots = cot.shape[0]
    odd = sub % 2
    near, far = sub + 1 - 2 * odd, sub - 1 + 2 * odd
    has_near = near < n_sub
    has_far = jnp.logical_and(far >= 0, far < n_sub)
    near_field, far_field = 1 - odd, odd
    has_above, has_below = lat > 0, lat < n_lat - 1

    loads = [(inc_hbm, raw.at[0]), (mul_hbm, raw.at[1]), (cols_hbm, cols), (cot_hbm, cot), (back_hbm, back),
             (hw_hbm, hw), (bias_hbm, bias), (ow_hbm, ow), (rates_hbm, rates)]
    loads = [pltpu.make_async_copy(a, b, load_sem.at[k]) for k, (a, b) in enumerate(loads)]
    for load in loads[:2]:
        load.start()

    barrier = pltpu.get_barrier_semaphore()
    near_above, near_below = jnp.logical_and(has_near, has_above), jnp.logical_and(has_near, has_below)
    others = [({"sub": near}, has_near), ({"sub": far}, has_far), ({"lat": lat - 1}, has_above), ({"lat": lat + 1}, has_below),
              ({"sub": near, "lat": lat - 1}, near_above), ({"sub": near, "lat": lat + 1}, near_below)]
    amount = sum(have.astype(jnp.int32) for _, have in others)
    for target, have in others:
        @pl.when(have)
        def _(target=target):
            pl.semaphore_signal(barrier, inc=1, device_id=target, device_id_type=MESH)
    if n_lon > 1:
        pl.semaphore_signal(barrier, inc=1, device_id={"lon": 1 - lon}, device_id_type=MESH)
        amount = amount + 1

    def copy(f, kind, src, dst, target):
        return pltpu.make_async_remote_copy(src_ref=src, dst_ref=dst, send_sem=send_sem.at[f, kind],
                                            recv_sem=recv_sem.at[f, kind], device_id=target, device_id_type=MESH)

    def center(f, part, target):
        return copy(f, CENTER + part, sent.at[f, pl.ds(part * HALO, HALO)],
                    field.at[f, pl.ds(HALO + part * HALO, HALO)], target)

    def upward(f):
        return copy(f, DOWN, field.at[f, pl.ds(HALO, HALO)], field.at[f, pl.ds(HALO + height, HALO)], {"lat": lat - 1})

    def downward(f):
        return copy(f, UP, field.at[f, pl.ds(height, HALO)], field.at[f, pl.ds(0, HALO)], {"lat": lat + 1})

    def direct(k):
        f, src, dst, row = ((far_field, 0, HALO + height, lat - 1), (far_field, height - HALO, 0, lat + 1))[k]
        return pltpu.make_async_remote_copy(
            src_ref=sent.at[f, pl.ds(src, HALO)], dst_ref=field.at[f, pl.ds(dst, HALO)],
            send_sem=send_sem.at[f, DIRECT + k], recv_sem=recv_sem.at[f, (DOWN, UP)[k]],
            device_id={"sub": near, "lat": row}, device_id_type=MESH)

    def sideways(f, k):
        lo, amount = ((HALO // 2, height // 2), (0, HALO // 2), ((HALO + height) // 2, HALO // 2))[k]
        return copy(f, SIDE + k, stage.at[f, pl.ds(lo, amount)], side.at[f, pl.ds(lo, amount)], {"lon": 1 - lon})

    def keep(f, k):
        lo, amount = ((HALO, height), (0, HALO), (HALO + height, HALO))[k]
        rows = pl.ds(lo, amount)
        return pltpu.make_async_copy(field.at[f, rows], field_out.at[rows], out_sem.at[k])

    def pass_on(f, k, stored=False):
        if stored:
            keep(f, k).start()
        if n_lon > 1:
            lo, amount = ((HALO // 2, height // 2), (0, HALO // 2), ((HALO + height) // 2, HALO // 2))[k]

            @pl.loop(lo, lo + amount)
            def _(p):
                pair = []
                for q in range(2):
                    row = field[f, 2 * p + q].astype(F32)
                    pair.append(jnp.where(lon == 0, row[across - HALO:], row[:HALO]))
                stage[f, p] = jnp.concatenate(pair, axis=0).astype(BF16)
            sideways(f, k).start()

    def take_near_center():
        center(near_field, 0, {"sub": near}).wait_recv()
        center(near_field, 1, {"sub": near}).wait_recv()
        pass_on(near_field, 0)

    def take_far_center():
        center(far_field, 0, {"sub": far}).wait_recv()

        @pl.when(has_above)
        def _():
            upward(far_field).start()
        center(far_field, 1, {"sub": far}).wait_recv()

        @pl.when(has_below)
        def _():
            downward(far_field).start()
        pass_on(far_field, 0, True)

    def take_halo(f, stored=False):
        @pl.when(has_above)
        def _():
            downward(f).wait_recv()
            pass_on(f, 1, stored)

        @pl.when(has_below)
        def _():
            upward(f).wait_recv()
            pass_on(f, 2, stored)

    def settle(f):
        if n_lon > 1:
            sideways(f, 0).wait()

            @pl.when(has_above)
            def _():
                sideways(f, 1).wait()

            @pl.when(has_below)
            def _():
                sideways(f, 2).wait()

    def cast(f):
        pltpu.make_async_copy(inc_hbm, raw.at[f], load_sem.at[f]).wait()
        for part in range(2):
            rows = pl.ds(part * HALO, HALO)
            sent[f, rows] = raw[f, rows].astype(BF16)

    cast(near_field)
    pl.semaphore_wait(barrier, amount)

    @pl.when(has_far)
    def _():
        for part in range(2):
            center(near_field, part, {"sub": far}).start()
    cast(far_field)

    @pl.when(near_above)
    def _():
        direct(0).start()

    @pl.when(near_below)
    def _():
        direct(1).start()

    @pl.when(has_near)
    def _():
        for part in range(2):
            center(far_field, part, {"sub": near}).start()

    for load in loads[2:]:
        load.start()
    for load in loads[2:]:
        load.wait()
    count = count_ref[lat * n_lon + lon]
    tile = 256
    chunks = slots // LANES
    place = (lax.broadcasted_iota(jnp.int32, (chunks, LANES), 0) * LANES
             + lax.broadcasted_iota(jnp.int32, (chunks, LANES), 1))
    slot_cols[...] = jnp.where(place < count, cols[...], -1)

    def adjoint_copy(t):
        rows = pl.ds(pl.multiple_of(t * tile, tile), tile)
        return pltpu.make_async_copy(adjoint.at[rows], adjoint_out.at[rows], adj_sem.at[t])

    def tangent_copy(t):
        rows = pl.ds(pl.multiple_of(t * tile, tile), tile)
        return pltpu.make_async_copy(tangent.at[rows], tangent_out.at[rows], tan_sem.at[t])

    def observe_columns(t):
        base = pl.multiple_of(t * tile, tile)
        rows = pl.ds(base, tile)
        wanted = lax.broadcasted_iota(jnp.int32, (tile, LANES), 0) + base
        hits = [jnp.where(slot_cols[k:k + 1, :] == wanted, 1.0, 0.0).astype(BF16) for k in range(chunks)]
        summed = dot(jnp.concatenate(hits, axis=1), cot[...]).astype(BF16)
        hidden = jnp.tanh(dot(back[rows, :], hw[...]) + bias[...])
        slopes = 1.0 - hidden * hidden
        state = sent[0, pl.ds(t * (tile // across), tile // across)].reshape(tile, levels)
        forward = dot(state, hw[...])
        per_column[rows, :] = dot((slopes * forward).astype(BF16), ow[...]).astype(BF16)
        pulled = dot_nt(summed, ow[...])
        adjoint[rows, :] = dot_nt((slopes * pulled).astype(BF16), hw[...])
        adjoint_copy(t).start()

    def observe_slots(t):
        parts = []
        for h in range(tile // LANES):
            named = jnp.transpose(jnp.broadcast_to(slot_cols[pl.ds(t * (tile // LANES) + h, 1), :], (LANES, LANES)))
            lane = lax.broadcasted_iota(jnp.int32, (LANES, LANES), 1)
            hits = [jnp.where(named == lane + c * LANES, 1.0, 0.0).astype(BF16) for c in range(columns // LANES)]
            parts.append(jnp.concatenate(hits, axis=1))
        tangent[pl.ds(pl.multiple_of(t * tile, tile), tile), :] = dot(
            jnp.concatenate(parts, axis=0), per_column[...]).astype(BF16)
        tangent_copy(t).start()

    def near_group(g):
        lanes = pl.ds(pl.multiple_of(g * LANES, LANES), LANES)
        start, side_at = lon_places(lon, n_lon, across)
        transport_field(lat == 0, lat == n_lat - 1, start, side_at, field, side, near_field, lanes, rates,
                        near_field == 0, window, one, two, n_lon)
        moved[:, :, lanes] = window[pl.ds(HALO, height), pl.ds(start, across), :]

    column_tiles, slot_tiles, groups = columns // tile, slots // tile, levels // LANES
    pl.loop(0, column_tiles // 2)(observe_columns)

    @pl.when(has_near)
    def _():
        take_near_center()
    pl.loop(column_tiles // 2, column_tiles)(observe_columns)

    @pl.when(has_far)
    def _():
        take_far_center()
    pl.loop(0, slot_tiles // 2)(observe_slots)

    @pl.when(has_near)
    def _():
        take_halo(near_field)
    pl.loop(slot_tiles // 2, slot_tiles)(observe_slots)

    @pl.when(has_near)
    def _():
        settle(near_field)

    @pl.loop(0, groups)
    def _(g):
        @pl.when(jnp.logical_and(has_far, g == groups // 2))
        def _():
            take_halo(far_field, True)

        @pl.when(has_near)
        def _():
            near_group(g)

    kept = [pltpu.make_async_copy(moved, moved_out, moved_sem)]
    kept[0].start()

    @pl.when(has_near)
    def _():
        for part in range(2):
            center(far_field, part, {"sub": near}).wait_send()

    @pl.when(near_above)
    def _():
        direct(0).wait_send()

    @pl.when(near_below)
    def _():
        direct(1).wait_send()

    @pl.when(has_far)
    def _():
        settle(far_field)
        for part in range(2):
            center(near_field, part, {"sub": far}).wait_send()
        keep(far_field, 0).wait()

        @pl.when(has_above)
        def _():
            upward(far_field).wait_send()
            keep(far_field, 1).wait()

        @pl.when(has_below)
        def _():
            downward(far_field).wait_send()
            keep(far_field, 2).wait()

    if n_lon > 1:
        kept.append(pltpu.make_async_copy(side.at[far_field], side_out, load_sem.at[0]))
        kept[1].start()
    for item in kept:
        item.wait()
    for t in range(column_tiles):
        adjoint_copy(t).wait()
    for t in range(slot_tiles):
        tangent_copy(t).wait()


def exchange(sizes, count, cols, inc, mul, back, cot, hw, bias, ow, rates):
    height, across, levels = inc.shape
    columns = height * across
    slots, chan = cot.shape
    hid = hw.shape[1]
    total = height + 2 * HALO
    anywhere = pl.BlockSpec(memory_space=pl.ANY)
    vm = pltpu.VMEM
    dma = pltpu.SemaphoreType.DMA
    field_shape, side_shape = (2, total, across, levels), (2, total // 2, 2 * HALO, levels)
    flops = 2 * columns * levels * hid * 5 + 4 * columns * slots * chan
    window, state = transport_scratch(inc.shape, sizes[2])
    return pl.pallas_call(
        functools.partial(exchange_kernel, sizes),
        out_shape=(jax.ShapeDtypeStruct(field_shape[1:], BF16), jax.ShapeDtypeStruct(side_shape[1:], BF16),
                   jax.ShapeDtypeStruct((slots, chan), BF16), jax.ShapeDtypeStruct((columns, levels), F32), jax.ShapeDtypeStruct(inc.shape, F32)),
        in_specs=[pl.BlockSpec(memory_space=pltpu.SMEM)] + [anywhere] * 9,
        out_specs=(anywhere,) * 5,
        scratch_shapes=[
            vm(rates.shape, F32), vm(inc.shape, F32), window, state, state,
            vm(cols.shape, jnp.int32), vm((2,) + inc.shape, F32), vm((2,) + inc.shape, BF16),
            vm(back.shape, BF16), vm(cot.shape, BF16), vm(hw.shape, BF16), vm(bias.shape, F32), vm(ow.shape, BF16),
            vm(field_shape, BF16), vm(side_shape, BF16), vm(side_shape, BF16),
            vm((columns, chan), BF16), vm(cols.shape, jnp.int32), vm((slots, chan), BF16), vm((columns, levels), F32),
            dma((9,)), dma((2, KINDS)), dma((2, KINDS)), dma((3,)), dma((slots // 256,)), dma((columns // 256,)), dma,
        ],
        compiler_params=pltpu.CompilerParams(vmem_limit_bytes=VMEM_BYTES, collective_id=0, has_side_effects=True),
        cost_estimate=pl.CostEstimate(flops=flops, bytes_accessed=20 << 20, transcendentals=columns * hid),
        name="exchange",
    )(count, cols, inc, mul, back, cot, hw, bias, ow, rates)


def lon_places(lon, n_lon, across):
    if n_lon == 1:
        return 0, 0
    first = lon == 0
    return pl.multiple_of(jnp.where(first, 0, HALO), HALO), pl.multiple_of(jnp.where(first, across, 0), HALO)


def transport_scratch(shape, n_lon):
    height, across, _ = shape
    width = (across + (HALO if n_lon > 1 else 0)) // SUB
    total = height + 2 * HALO
    return (pltpu.VMEM((total, width * SUB, LANES), F32),
            pltpu.VMEM((total, width + 2 * REACH, SUB, LANES), F32))


def transport_field(lat_first, lat_last, start, side_at, field, side, f, lanes, rates, is_ahead, window, one, two, n_lon):
    total, width = window.shape[0], window.shape[1] // SUB
    across = field.shape[2]

    @pl.loop(0, total // 2)
    def _(p):
        if n_lon > 1:
            pair = side[f, p, :, lanes].astype(F32)
        for q in range(2):
            window[2 * p + q, pl.ds(start, across), :] = field[f, 2 * p + q, :, lanes].astype(F32)
            if n_lon > 1:
                window[2 * p + q, pl.ds(side_at, HALO), :] = pair[q * HALO:(q + 1) * HALO]

    lane_row = lax.broadcasted_iota(jnp.int32, (SUB, LANES), 0)
    low_edge = lane_row == 0
    high_edge = lane_row == SUB - 1

    def put(ref, r, v, vec):
        ref[r, v + REACH] = vec
        if v >= width - REACH:
            ref[r, v - (width - REACH)] = jnp.where(low_edge, 0.0, pltpu.roll(vec, 1, 0))
        if v < REACH:
            ref[r, v + width + REACH] = jnp.where(high_edge, 0.0, pltpu.roll(vec, SUB - 1, 0))

    def clear_outside(ref):
        zero = jnp.zeros((HALO,) + ref.shape[1:], F32)

        @pl.when(lat_first)
        def _():
            ref[pl.ds(0, HALO)] = zero

        @pl.when(lat_last)
        def _():
            ref[pl.ds(total - HALO, HALO)] = zero

    @pl.loop(0, total // 2)
    def _(p):
        for q in range(2):
            for v in range(width):
                put(one, 2 * p + q, v, window[2 * p + q, pl.ds(v, SUB, stride=width), :])
    clear_outside(one)

    c = [jnp.where(is_ahead, rates[k:k + 1, lanes], rates[m:m + 1, lanes]) for k, m in enumerate((3, 2, 1, 0, 7, 6, 5, 4))]
    c.append(1.0 - (((c[0] + c[1]) + (c[2] + c[3])) + ((c[4] + c[5]) + (c[6] + c[7]))))
    c = [jnp.broadcast_to(x, (SUB, LANES)) for x in c]
    for step in range(STEPS):
        src, dst = (one, two) if step % 2 == 0 else (two, one)
        lo = REACH * (step + 1)

        @pl.loop(0, (total - 2 * lo) // BLOCK)
        def _(b):
            r = lo + b * BLOCK
            lines = [[src[r + q, k] for k in range(2 * REACH)] for q in range(BLOCK)]
            for v in range(width):
                for q in range(BLOCK):
                    lines[q].append(src[r + q, v + 2 * REACH])
                tall = ([src[r + k - REACH, v + REACH] for k in range(REACH)] + [line[v + REACH] for line in lines]
                        + [src[r + BLOCK + k, v + REACH] for k in range(REACH)])
                for q in range(BLOCK):
                    line = lines[q][v:v + 2 * REACH + 1]
                    acc = ((c[8] * tall[q + 2] + c[0] * tall[q]) + (c[1] * tall[q + 1] + c[2] * tall[q + 3])
                           + (c[3] * tall[q + 4] + c[5] * line[1])
                           + ((c[4] * line[0] + c[6] * line[3]) + c[7] * line[4]))
                    if step == STEPS - 1:
                        window[r + q, pl.ds(v, SUB, stride=width), :] = acc
                    else:
                        put(dst, r + q, v, acc)
        if step < STEPS - 1:
            clear_outside(dst)


def transport_kernel(sizes, rates, field, side, moved, inc_ref, mul_ref, adj_ref, err_ref, grad_ref, window, one, two):
    n_sub, n_lat, n_lon = sizes
    sub, lat, lon = lax.axis_index("sub"), lax.axis_index("lat"), lax.axis_index("lon")
    height, across = inc_ref.shape[0], inc_ref.shape[1]
    start, side_at = lon_places(lon, n_lon, across)
    odd = sub % 2
    far_is_ahead = odd == 0
    near = sub + 1 - 2 * odd
    far = sub - 1 + 2 * odd
    result = (pl.ds(HALO, height), pl.ds(start, across))

    @pl.when(jnp.logical_and(far >= 0, far < n_sub))
    def _():
        transport_field(lat == 0, lat == n_lat - 1, start, side_at, field, side, 0, slice(None), rates,
                        far_is_ahead, window, one, two, n_lon)

    @pl.when(jnp.logical_or(far < 0, far >= n_sub))
    def _():
        window[...] = jnp.zeros_like(window)
    near_part = jnp.where(near < n_sub, moved[...], 0.0)
    far_part = window[result]
    err_ref[...] = inc_ref[...] - jnp.where(far_is_ahead, far_part, near_part)
    grad_ref[...] = mul_ref[...] - jnp.where(far_is_ahead, near_part, far_part) + adj_ref[...]


def transport_call(sizes, rates, field, side, moved, inc, mul, adj):
    height, across, levels = inc.shape

    def whole(shape):
        return pl.BlockSpec(shape[:-1] + (LANES,), lambda g: (0,) * (len(shape) - 1) + (g,))
    arrays = (rates, field[None], side[None], moved, inc, mul, adj)
    window, state = transport_scratch(inc.shape, sizes[2])
    return pl.pallas_call(
        functools.partial(transport_kernel, sizes),
        grid=(levels // LANES,),
        out_shape=(jax.ShapeDtypeStruct(inc.shape, F32),) * 2,
        in_specs=[whole(x.shape) for x in arrays],
        out_specs=(whole(inc.shape),) * 2,
        scratch_shapes=[window, state, state],
        compiler_params=pltpu.CompilerParams(vmem_limit_bytes=VMEM_BYTES),
        cost_estimate=pl.CostEstimate(flops=4 * 17 * height * across * levels, bytes_accessed=16 << 20, transcendentals=0),
        name="transport",
    )(*arrays)


def local(increment, multiplier, background, obs_cotangent, obs_column, obs_count, transport,
          hidden_weight, hidden_bias, output_weight):
    sizes = tuple(lax.axis_size(name) for name in ("sub", "lat", "lon"))
    assert sizes[2] <= 2
    inc, mul = increment[0], multiplier[0]
    levels = inc.shape[-1]
    field, side, tangent, adj, moved = exchange(
        sizes, obs_count[0], obs_column.reshape(-1, LANES), inc, mul, background.reshape(-1, levels),
        obs_cotangent[0, 0], hidden_weight, hidden_bias[None], output_weight, transport)
    err, grad = transport_call(sizes, transport, field, side, moved, inc, mul, adj.reshape(inc.shape))
    return err[None], grad[None], tangent[None, None]


def solution(mesh):
    field = P("sub", "lat", "lon", None)
    slots = P("sub", ("lat", "lon"), None, None)
    in_specs = (field, field, field, slots, P("sub", ("lat", "lon"), None), P("sub", None), P(), P(), P(), P())
    return jax.shard_map(local, mesh=mesh, in_specs=in_specs, out_specs=(field, field, slots), check_vma=False)
```

```python
import functools

import jax
import jax.numpy as jnp
from jax import lax
from jax.experimental import pallas as pl
from jax.experimental.pallas import tpu as pltpu
from jax.sharding import PartitionSpec as P

STEPS = 4
REACH = 2
HALO = STEPS * REACH
SUB = 8
LANES = 128
PAIR = 2
TILE = 512
WIDE = PAIR * LANES
BLOCK = 4
MESH = pl.DeviceIdType.MESH
NT = (((1,), (1,)), ((), ()))
F32 = jnp.float32
BF16 = jnp.bfloat16


def dot(a, b):
    return jnp.dot(a, b, preferred_element_type=F32)


def dot_nt(a, b):
    return lax.dot_general(a, b, NT, preferred_element_type=F32)


CENTER, UP, DOWN, SIDE = 0, 2, 3, 4
DIRECT = 7
KINDS = 9
VMEM_BYTES = 58 << 20


def exchange_kernel(sizes, count_ref, cols_hbm, inc_hbm, mul_hbm, back_hbm, cot_hbm, hw_hbm, bias_hbm, ow_hbm, rates_hbm,
                    field_out, side_out, tangent_out, adjoint_out, moved_out,
                    rates, moved, window, one, two, cols, raw, sent, back, cot, hw, bias, ow, field, side, stage,
                    per_column, slot_cols, tangent, adjoint,
                    load_sem, send_sem, recv_sem, out_sem, tan_sem, adj_sem, moved_sem):
    n_sub, n_lat, n_lon = sizes
    sub, lat, lon = lax.axis_index("sub"), lax.axis_index("lat"), lax.axis_index("lon")
    height, across, levels = inc_hbm.shape
    columns = height * across
    slots = cot.shape[0]
    odd = sub % 2
    near, far = sub + 1 - 2 * odd, sub - 1 + 2 * odd
    has_near = near < n_sub
    has_far = jnp.logical_and(far >= 0, far < n_sub)
    near_field, far_field = 1 - odd, odd
    has_above, has_below = lat > 0, lat < n_lat - 1

    loads = [(inc_hbm, raw.at[0]), (mul_hbm, raw.at[1]), (cols_hbm, cols), (cot_hbm, cot), (back_hbm, back),
             (hw_hbm, hw), (bias_hbm, bias), (ow_hbm, ow), (rates_hbm, rates)]
    loads = [pltpu.make_async_copy(a, b, load_sem.at[k]) for k, (a, b) in enumerate(loads)]
    for load in loads[:2]:
        load.start()

    barrier = pltpu.get_barrier_semaphore()
    near_above, near_below = jnp.logical_and(has_near, has_above), jnp.logical_and(has_near, has_below)
    others = [({"sub": near}, has_near), ({"sub": far}, has_far), ({"lat": lat - 1}, has_above), ({"lat": lat + 1}, has_below),
              ({"sub": near, "lat": lat - 1}, near_above), ({"sub": near, "lat": lat + 1}, near_below)]
    amount = sum(have.astype(jnp.int32) for _, have in others)
    for target, have in others:
        @pl.when(have)
        def _(target=target):
            pl.semaphore_signal(barrier, inc=1, device_id=target, device_id_type=MESH)
    if n_lon > 1:
        pl.semaphore_signal(barrier, inc=1, device_id={"lon": 1 - lon}, device_id_type=MESH)
        amount = amount + 1

    def copy(f, kind, src, dst, target):
        return pltpu.make_async_remote_copy(src_ref=src, dst_ref=dst, send_sem=send_sem.at[f, kind],
                                            recv_sem=recv_sem.at[f, kind], device_id=target, device_id_type=MESH)

    def center(f, part, target):
        return copy(f, CENTER + part, sent.at[f, pl.ds(part * HALO, HALO)],
                    field.at[f, pl.ds(HALO + part * HALO, HALO)], target)

    def upward(f):
        return copy(f, DOWN, field.at[f, pl.ds(HALO, HALO)], field.at[f, pl.ds(HALO + height, HALO)], {"lat": lat - 1})

    def downward(f):
        return copy(f, UP, field.at[f, pl.ds(height, HALO)], field.at[f, pl.ds(0, HALO)], {"lat": lat + 1})

    def direct(k):
        f, src, dst, row = ((far_field, 0, HALO + height, lat - 1), (far_field, height - HALO, 0, lat + 1))[k]
        return pltpu.make_async_remote_copy(
            src_ref=sent.at[f, pl.ds(src, HALO)], dst_ref=field.at[f, pl.ds(dst, HALO)],
            send_sem=send_sem.at[f, DIRECT + k], recv_sem=recv_sem.at[f, (DOWN, UP)[k]],
            device_id={"sub": near, "lat": row}, device_id_type=MESH)

    def sideways(f, k):
        lo, amount = ((HALO // 2, height // 2), (0, HALO // 2), ((HALO + height) // 2, HALO // 2))[k]
        return copy(f, SIDE + k, stage.at[f, pl.ds(lo, amount)], side.at[f, pl.ds(lo, amount)], {"lon": 1 - lon})

    def keep(f, k):
        lo, amount = ((HALO, height), (0, HALO), (HALO + height, HALO))[k]
        rows = pl.ds(lo, amount)
        return pltpu.make_async_copy(field.at[f, rows], field_out.at[rows], out_sem.at[k])

    def pass_on(f, k, stored=False):
        if stored:
            keep(f, k).start()
        if n_lon > 1:
            lo, amount = ((HALO // 2, height // 2), (0, HALO // 2), ((HALO + height) // 2, HALO // 2))[k]

            @pl.loop(lo, lo + amount)
            def _(p):
                pair = []
                for q in range(2):
                    row = field[f, 2 * p + q].astype(F32)
                    pair.append(jnp.where(lon == 0, row[across - HALO:], row[:HALO]))
                stage[f, p] = jnp.concatenate(pair, axis=0).astype(BF16)
            sideways(f, k).start()

    def take_near_center():
        center(near_field, 0, {"sub": near}).wait_recv()
        center(near_field, 1, {"sub": near}).wait_recv()
        pass_on(near_field, 0)

    def take_far_center():
        center(far_field, 0, {"sub": far}).wait_recv()

        @pl.when(has_above)
        def _():
            upward(far_field).start()
        center(far_field, 1, {"sub": far}).wait_recv()

        @pl.when(has_below)
        def _():
            downward(far_field).start()
        pass_on(far_field, 0, True)

    def take_halo(f, stored=False):
        @pl.when(has_above)
        def _():
            downward(f).wait_recv()
            pass_on(f, 1, stored)

        @pl.when(has_below)
        def _():
            upward(f).wait_recv()
            pass_on(f, 2, stored)

    def settle(f):
        if n_lon > 1:
            sideways(f, 0).wait()

            @pl.when(has_above)
            def _():
                sideways(f, 1).wait()

            @pl.when(has_below)
            def _():
                sideways(f, 2).wait()

    def cast(f):
        for part in range(2):
            rows = pl.ds(part * HALO, HALO)
            sent[f, rows] = raw[f, rows].astype(BF16)

    for load in loads[:2]:
        load.wait()
    for load in loads[2:]:
        load.start()
    cast(near_field)
    pl.semaphore_wait(barrier, amount)

    @pl.when(has_far)
    def _():
        for part in range(2):
            center(near_field, part, {"sub": far}).start()
    cast(far_field)

    @pl.when(near_above)
    def _():
        direct(0).start()

    @pl.when(near_below)
    def _():
        direct(1).start()

    @pl.when(has_near)
    def _():
        for part in range(2):
            center(far_field, part, {"sub": near}).start()

    for load in loads[2:]:
        load.wait()
    count = count_ref[lat * n_lon + lon]
    tile = TILE
    chunks = slots // LANES
    place = (lax.broadcasted_iota(jnp.int32, (chunks, LANES), 0) * LANES
             + lax.broadcasted_iota(jnp.int32, (chunks, LANES), 1))
    slot_cols[...] = jnp.where(place < count, cols[...], -1)

    def adjoint_copy(t):
        rows = pl.ds(pl.multiple_of(t * tile, tile), tile)
        return pltpu.make_async_copy(adjoint.at[rows], adjoint_out.at[rows], adj_sem.at[t])

    def tangent_copy(t):
        rows = pl.ds(pl.multiple_of(t * tile, tile), tile)
        return pltpu.make_async_copy(tangent.at[rows], tangent_out.at[rows], tan_sem.at[t])

    def observe_columns(t):
        base = pl.multiple_of(t * tile, tile)
        rows = pl.ds(base, tile)
        wanted = lax.broadcasted_iota(jnp.int32, (tile, LANES), 0) + base
        hits = [jnp.where(slot_cols[k:k + 1, :] == wanted, 1.0, 0.0).astype(BF16) for k in range(chunks)]
        summed = dot(jnp.concatenate(hits, axis=1), cot[...]).astype(BF16)
        hidden = jnp.tanh(dot(back[rows, :], hw[...]) + bias[...])
        slopes = 1.0 - hidden * hidden
        state = sent[0, pl.ds(t * (tile // across), tile // across)].reshape(tile, levels)
        forward = dot(state, hw[...])
        per_column[rows, :] = dot((slopes * forward).astype(BF16), ow[...]).astype(BF16)
        pulled = dot_nt(summed, ow[...])
        adjoint[rows, :] = dot_nt((slopes * pulled).astype(BF16), hw[...])
        adjoint_copy(t).start()

    def observe_slots(t):
        parts = []
        for h in range(tile // LANES):
            named = jnp.transpose(jnp.broadcast_to(slot_cols[pl.ds(t * (tile // LANES) + h, 1), :], (LANES, LANES)))
            lane = lax.broadcasted_iota(jnp.int32, (LANES, LANES), 1)
            hits = [jnp.where(named == lane + c * LANES, 1.0, 0.0).astype(BF16) for c in range(columns // LANES)]
            parts.append(jnp.concatenate(hits, axis=1))
        tangent[pl.ds(pl.multiple_of(t * tile, tile), tile), :] = dot(
            jnp.concatenate(parts, axis=0), per_column[...]).astype(BF16)
        tangent_copy(t).start()

    def near_group(g):
        lanes = [pl.ds(pl.multiple_of(g * WIDE + h * LANES, LANES), LANES) for h in range(PAIR)]
        start, side_at = lon_places(lon, n_lon, across)
        transport_field(lat == 0, lat == n_lat - 1, start, side_at, field, side, near_field, lanes, rates,
                        near_field == 0, window, one, two, n_lon)
        for h in range(PAIR):
            moved[:, :, lanes[h]] = window[h, pl.ds(HALO, height), pl.ds(start, across), :]

    column_tiles, slot_tiles, groups = columns // tile, slots // tile, levels // WIDE
    pl.loop(0, column_tiles // 2)(observe_columns)

    @pl.when(has_near)
    def _():
        take_near_center()
    pl.loop(column_tiles // 2, column_tiles)(observe_columns)

    @pl.when(has_far)
    def _():
        take_far_center()
    pl.loop(0, slot_tiles // 2)(observe_slots)

    @pl.when(has_near)
    def _():
        take_halo(near_field)
    pl.loop(slot_tiles // 2, slot_tiles)(observe_slots)

    @pl.when(has_near)
    def _():
        settle(near_field)

    @pl.loop(0, groups)
    def _(g):
        @pl.when(jnp.logical_and(has_far, g == groups // 2))
        def _():
            take_halo(far_field, True)

        @pl.when(has_near)
        def _():
            near_group(g)

    kept = [pltpu.make_async_copy(moved, moved_out, moved_sem)]
    kept[0].start()

    @pl.when(has_near)
    def _():
        for part in range(2):
            center(far_field, part, {"sub": near}).wait_send()

    @pl.when(near_above)
    def _():
        direct(0).wait_send()

    @pl.when(near_below)
    def _():
        direct(1).wait_send()

    @pl.when(has_far)
    def _():
        settle(far_field)
        for part in range(2):
            center(near_field, part, {"sub": far}).wait_send()
        keep(far_field, 0).wait()

        @pl.when(has_above)
        def _():
            upward(far_field).wait_send()
            keep(far_field, 1).wait()

        @pl.when(has_below)
        def _():
            downward(far_field).wait_send()
            keep(far_field, 2).wait()

    if n_lon > 1:
        kept.append(pltpu.make_async_copy(side.at[far_field], side_out, load_sem.at[0]))
        kept[1].start()
    for item in kept:
        item.wait()
    for t in range(column_tiles):
        adjoint_copy(t).wait()
    for t in range(slot_tiles):
        tangent_copy(t).wait()


def exchange(sizes, count, cols, inc, mul, back, cot, hw, bias, ow, rates):
    height, across, levels = inc.shape
    columns = height * across
    slots, chan = cot.shape
    hid = hw.shape[1]
    total = height + 2 * HALO
    anywhere = pl.BlockSpec(memory_space=pl.ANY)
    vm = pltpu.VMEM
    dma = pltpu.SemaphoreType.DMA
    field_shape, side_shape = (2, total, across, levels), (2, total // 2, 2 * HALO, levels)
    flops = 2 * columns * levels * hid * 5 + 4 * columns * slots * chan
    window, state = transport_scratch(inc.shape, sizes[2])
    return pl.pallas_call(
        functools.partial(exchange_kernel, sizes),
        out_shape=(jax.ShapeDtypeStruct(field_shape[1:], BF16), jax.ShapeDtypeStruct(side_shape[1:], BF16),
                   jax.ShapeDtypeStruct((slots, chan), BF16), jax.ShapeDtypeStruct((columns, levels), F32), jax.ShapeDtypeStruct(inc.shape, F32)),
        in_specs=[pl.BlockSpec(memory_space=pltpu.SMEM)] + [anywhere] * 9,
        out_specs=(anywhere,) * 5,
        scratch_shapes=[
            vm(rates.shape, F32), vm(inc.shape, F32), window, state, state,
            vm(cols.shape, jnp.int32), vm((2,) + inc.shape, F32), vm((2,) + inc.shape, BF16),
            vm(back.shape, BF16), vm(cot.shape, BF16), vm(hw.shape, BF16), vm(bias.shape, F32), vm(ow.shape, BF16),
            vm(field_shape, BF16), vm(side_shape, BF16), vm(side_shape, BF16),
            vm((columns, chan), BF16), vm(cols.shape, jnp.int32), vm((slots, chan), BF16), vm((columns, levels), F32),
            dma((9,)), dma((2, KINDS)), dma((2, KINDS)), dma((3,)), dma((slots // TILE,)), dma((columns // TILE,)), dma,
        ],
        compiler_params=pltpu.CompilerParams(vmem_limit_bytes=VMEM_BYTES, collective_id=0, has_side_effects=True),
        cost_estimate=pl.CostEstimate(flops=flops, bytes_accessed=20 << 20, transcendentals=columns * hid),
        name="exchange",
    )(count, cols, inc, mul, back, cot, hw, bias, ow, rates)


def lon_places(lon, n_lon, across):
    if n_lon == 1:
        return 0, 0
    first = lon == 0
    return pl.multiple_of(jnp.where(first, 0, HALO), HALO), pl.multiple_of(jnp.where(first, across, 0), HALO)


def transport_scratch(shape, n_lon):
    height, across, _ = shape
    width = (across + (HALO if n_lon > 1 else 0)) // SUB
    total = height + 2 * HALO
    return (pltpu.VMEM((PAIR, total, width * SUB, LANES), F32),
            pltpu.VMEM((PAIR, total, width + 2 * REACH, SUB, LANES), F32))


def transport_field(lat_first, lat_last, start, side_at, field, side, f, lanes, rates, is_ahead, window, one, two, n_lon):
    total, width = window.shape[1], window.shape[2] // SUB
    across = field.shape[2]
    lane_row = lax.broadcasted_iota(jnp.int32, (SUB, LANES), 0)
    low_edge = lane_row == 0
    high_edge = lane_row == SUB - 1

    def put(ref, h, r, v, vec):
        ref[h, r, v + REACH] = vec
        if v >= width - REACH:
            ref[h, r, v - (width - REACH)] = jnp.where(low_edge, 0.0, pltpu.roll(vec, 1, 0))
        if v < REACH:
            ref[h, r, v + width + REACH] = jnp.where(high_edge, 0.0, pltpu.roll(vec, SUB - 1, 0))

    def clear_outside(ref):
        zero = jnp.zeros((PAIR, HALO) + ref.shape[2:], F32)

        @pl.when(lat_first)
        def _():
            ref[:, pl.ds(0, HALO)] = zero

        @pl.when(lat_last)
        def _():
            ref[:, pl.ds(total - HALO, HALO)] = zero

    def fill(h, p):
        if n_lon > 1:
            pair = side[f, p, :, lanes[h]].astype(F32)
        for q in range(2):
            window[h, 2 * p + q, pl.ds(start, across), :] = field[f, 2 * p + q, :, lanes[h]].astype(F32)
            if n_lon > 1:
                window[h, 2 * p + q, pl.ds(side_at, HALO), :] = pair[q * HALO:(q + 1) * HALO]

    @pl.loop(0, total // 2)
    def _(p):
        for h in range(PAIR):
            fill(h, p)

    @pl.loop(0, total // 2)
    def _(p):
        for h in range(PAIR):
            for q in range(2):
                for v in range(width):
                    put(one, h, 2 * p + q, v, window[h, 2 * p + q, pl.ds(v, SUB, stride=width), :])
    clear_outside(one)

    coeffs = []
    for h in range(PAIR):
        c = [jnp.where(is_ahead, rates[k:k + 1, lanes[h]], rates[m:m + 1, lanes[h]])
             for k, m in enumerate((3, 2, 1, 0, 7, 6, 5, 4))]
        rest = 1.0 - (((c[0] + c[1]) + (c[2] + c[3])) + ((c[4] + c[5]) + (c[6] + c[7])))
        scale = 1.0 / rest
        square = rest * rest
        coeffs.append([jnp.broadcast_to(x, (SUB, LANES)) for x in [x * scale for x in c] + [square * square]])

    def advance(src, dst, h, r, last):
        c = coeffs[h]
        lines = [[src[h, r + q, k] for k in range(2 * REACH)] for q in range(BLOCK)]
        for v in range(width):
            for q in range(BLOCK):
                lines[q].append(src[h, r + q, v + 2 * REACH])
            tall = ([src[h, r + k - REACH, v + REACH] for k in range(REACH)] + [line[v + REACH] for line in lines]
                    + [src[h, r + BLOCK + k, v + REACH] for k in range(REACH)])
            for q in range(BLOCK):
                line = lines[q][v:v + 2 * REACH + 1]
                acc = ((tall[q + 2] + c[0] * tall[q]) + (c[1] * tall[q + 1] + c[2] * tall[q + 3])
                       + (c[3] * tall[q + 4] + c[5] * line[1])
                       + ((c[4] * line[0] + c[6] * line[3]) + c[7] * line[4]))
                if last:
                    window[h, r + q, pl.ds(v, SUB, stride=width), :] = acc * c[8]
                else:
                    put(dst, h, r + q, v, acc)

    for step in range(STEPS):
        src, dst = (one, two) if step % 2 == 0 else (two, one)
        lo = REACH * (step + 1)

        @pl.loop(0, (total - 2 * lo) // BLOCK)
        def _(b):
            for h in range(PAIR):
                advance(src, dst, h, lo + b * BLOCK, step == STEPS - 1)
        if step < STEPS - 1:
            clear_outside(dst)


def transport_kernel(sizes, rates, field, side, moved, inc_ref, mul_ref, adj_ref, tangent, err_ref, grad_ref, tangent_out,
                     window, one, two, tan_sem):
    n_sub, n_lat, n_lon = sizes
    sub, lat, lon = lax.axis_index("sub"), lax.axis_index("lat"), lax.axis_index("lon")
    height, across = inc_ref.shape[0], inc_ref.shape[1]
    start, side_at = lon_places(lon, n_lon, across)
    odd = sub % 2
    far_is_ahead = odd == 0
    near = sub + 1 - 2 * odd
    far = sub - 1 + 2 * odd
    result = (pl.ds(HALO, height), pl.ds(start, across))
    lanes = [slice(h * LANES, (h + 1) * LANES) for h in range(PAIR)]
    tangent_copy = pltpu.make_async_copy(tangent, tangent_out, tan_sem)

    @pl.when(pl.program_id(0) == 0)
    def _():
        tangent_copy.start()

    @pl.when(jnp.logical_and(far >= 0, far < n_sub))
    def _():
        transport_field(lat == 0, lat == n_lat - 1, start, side_at, field, side, 0, lanes, rates,
                        far_is_ahead, window, one, two, n_lon)

    @pl.when(jnp.logical_or(far < 0, far >= n_sub))
    def _():
        window[...] = jnp.zeros_like(window)
    for h in range(PAIR):
        part = (slice(None), slice(None), lanes[h])
        near_part = jnp.where(near < n_sub, moved[part], 0.0)
        far_part = window[(h,) + result]
        err_ref[part] = inc_ref[part] - jnp.where(far_is_ahead, far_part, near_part)
        grad_ref[part] = mul_ref[part] - jnp.where(far_is_ahead, near_part, far_part) + adj_ref[part]

    @pl.when(pl.program_id(0) == pl.num_programs(0) - 1)
    def _():
        tangent_copy.wait()


def transport_call(sizes, rates, field, side, moved, inc, mul, adj, tangent):
    height, across, levels = inc.shape

    def whole(shape):
        return pl.BlockSpec(shape[:-1] + (WIDE,), lambda g: (0,) * (len(shape) - 1) + (g,))
    anywhere = pl.BlockSpec(memory_space=pl.ANY)
    arrays = (rates, field[None], side[None], moved, inc, mul, adj)
    window, state = transport_scratch(inc.shape, sizes[2])
    return pl.pallas_call(
        functools.partial(transport_kernel, sizes),
        grid=(levels // WIDE,),
        out_shape=(jax.ShapeDtypeStruct(inc.shape, F32),) * 2 + (jax.ShapeDtypeStruct(tangent.shape, BF16),),
        in_specs=[whole(x.shape) for x in arrays] + [anywhere],
        out_specs=(whole(inc.shape),) * 2 + (anywhere,),
        scratch_shapes=[window, state, state, pltpu.SemaphoreType.DMA],
        compiler_params=pltpu.CompilerParams(vmem_limit_bytes=VMEM_BYTES),
        cost_estimate=pl.CostEstimate(flops=4 * 17 * height * across * levels, bytes_accessed=16 << 20, transcendentals=0),
        name="transport",
    )(*arrays, tangent)


def local(increment, multiplier, background, obs_cotangent, obs_column, obs_count, transport,
          hidden_weight, hidden_bias, output_weight):
    sizes = tuple(lax.axis_size(name) for name in ("sub", "lat", "lon"))
    assert sizes[2] <= 2
    inc, mul = increment[0], multiplier[0]
    levels = inc.shape[-1]
    field, side, tangent, adj, moved = exchange(
        sizes, obs_count[0], obs_column.reshape(-1, LANES), inc, mul, background.reshape(-1, levels),
        obs_cotangent[0, 0], hidden_weight, hidden_bias[None], output_weight, transport)
    err, grad, tangent = transport_call(sizes, transport, field, side, moved, inc, mul, adj.reshape(inc.shape), tangent)
    return err[None], grad[None], tangent[None, None]


def solution(mesh):
    field = P("sub", "lat", "lon", None)
    slots = P("sub", ("lat", "lon"), None, None)
    in_specs = (field, field, field, slots, P("sub", ("lat", "lon"), None), P("sub", None), P(), P(), P(), P())
    return jax.shard_map(local, mesh=mesh, in_specs=in_specs, out_specs=(field, field, slots), check_vma=False)
```

```python
import functools

import jax
import jax.numpy as jnp
from jax import lax
from jax.experimental import pallas as pl
from jax.experimental.pallas import tpu as pltpu
from jax.sharding import PartitionSpec as P

STEPS = 4
REACH = 2
HALO = STEPS * REACH
SUB = 8
LANES = 128
PAIR = 2
TILE = 512
WIDE = PAIR * LANES
BLOCK = 4
MESH = pl.DeviceIdType.MESH
NT = (((1,), (1,)), ((), ()))
F32 = jnp.float32
BF16 = jnp.bfloat16


def dot(a, b):
    return jnp.dot(a, b, preferred_element_type=F32)


def dot_nt(a, b):
    return lax.dot_general(a, b, NT, preferred_element_type=F32)


CENTER, UP, DOWN, SIDE = 0, 2, 3, 4
DIRECT = 7
KINDS = 9
VMEM_BYTES = 58 << 20


def exchange_kernel(sizes, count_ref, cols_hbm, inc_hbm, mul_hbm, back_hbm, cot_hbm, hw_hbm, bias_hbm, ow_hbm, rates_hbm,
                    field_out, side_out, tangent_out, adjoint_out, moved_out,
                    rates, moved, window, one, two, cols, raw, sent, back, cot, hw, bias, ow, field, side, stage,
                    per_column, slot_cols, tangent, adjoint,
                    load_sem, send_sem, recv_sem, out_sem, tan_sem, adj_sem, moved_sem):
    n_sub, n_lat, n_lon = sizes
    sub, lat, lon = lax.axis_index("sub"), lax.axis_index("lat"), lax.axis_index("lon")
    height, across, levels = inc_hbm.shape
    columns = height * across
    slots = cot.shape[0]
    odd = sub % 2
    near, far = sub + 1 - 2 * odd, sub - 1 + 2 * odd
    has_near = near < n_sub
    has_far = jnp.logical_and(far >= 0, far < n_sub)
    near_field, far_field = 1 - odd, odd
    has_above, has_below = lat > 0, lat < n_lat - 1

    loads = [(inc_hbm, raw.at[0]), (mul_hbm, raw.at[1]), (cols_hbm, cols), (cot_hbm, cot), (back_hbm, back),
             (hw_hbm, hw), (bias_hbm, bias), (ow_hbm, ow), (rates_hbm, rates)]
    loads = [pltpu.make_async_copy(a, b, load_sem.at[k]) for k, (a, b) in enumerate(loads)]
    for load in loads[:2]:
        load.start()

    barrier = pltpu.get_barrier_semaphore()
    near_above, near_below = jnp.logical_and(has_near, has_above), jnp.logical_and(has_near, has_below)
    others = [({"sub": near}, has_near), ({"sub": far}, has_far), ({"lat": lat - 1}, has_above), ({"lat": lat + 1}, has_below),
              ({"sub": near, "lat": lat - 1}, near_above), ({"sub": near, "lat": lat + 1}, near_below)]
    amount = sum(have.astype(jnp.int32) for _, have in others)
    for target, have in others:
        @pl.when(have)
        def _(target=target):
            pl.semaphore_signal(barrier, inc=1, device_id=target, device_id_type=MESH)
    if n_lon > 1:
        pl.semaphore_signal(barrier, inc=1, device_id={"lon": 1 - lon}, device_id_type=MESH)
        amount = amount + 1

    def copy(f, kind, src, dst, target):
        return pltpu.make_async_remote_copy(src_ref=src, dst_ref=dst, send_sem=send_sem.at[f, kind],
                                            recv_sem=recv_sem.at[f, kind], device_id=target, device_id_type=MESH)

    def center(f, part, target):
        return copy(f, CENTER + part, sent.at[f, pl.ds(part * HALO, HALO)],
                    field.at[f, pl.ds(HALO + part * HALO, HALO)], target)

    def upward(f):
        return copy(f, DOWN, field.at[f, pl.ds(HALO, HALO)], field.at[f, pl.ds(HALO + height, HALO)], {"lat": lat - 1})

    def downward(f):
        return copy(f, UP, field.at[f, pl.ds(height, HALO)], field.at[f, pl.ds(0, HALO)], {"lat": lat + 1})

    def direct(k):
        f, src, dst, row = ((far_field, 0, HALO + height, lat - 1), (far_field, height - HALO, 0, lat + 1))[k]
        return pltpu.make_async_remote_copy(
            src_ref=sent.at[f, pl.ds(src, HALO)], dst_ref=field.at[f, pl.ds(dst, HALO)],
            send_sem=send_sem.at[f, DIRECT + k], recv_sem=recv_sem.at[f, (DOWN, UP)[k]],
            device_id={"sub": near, "lat": row}, device_id_type=MESH)

    def sideways(f, k):
        lo, amount = ((HALO // 2, height // 2), (0, HALO // 2), ((HALO + height) // 2, HALO // 2))[k]
        return copy(f, SIDE + k, stage.at[f, pl.ds(lo, amount)], side.at[f, pl.ds(lo, amount)], {"lon": 1 - lon})

    def keep(f, k):
        lo, amount = ((HALO, height), (0, HALO), (HALO + height, HALO))[k]
        rows = pl.ds(lo, amount)
        return pltpu.make_async_copy(field.at[f, rows], field_out.at[rows], out_sem.at[k])

    def pass_on(f, k, stored=False):
        if stored:
            keep(f, k).start()
        if n_lon > 1:
            lo, amount = ((HALO // 2, height // 2), (0, HALO // 2), ((HALO + height) // 2, HALO // 2))[k]

            @pl.loop(lo, lo + amount)
            def _(p):
                pair = []
                for q in range(2):
                    row = field[f, 2 * p + q].astype(F32)
                    pair.append(jnp.where(lon == 0, row[across - HALO:], row[:HALO]))
                stage[f, p] = jnp.concatenate(pair, axis=0).astype(BF16)
            sideways(f, k).start()

    def take_near_center():
        center(near_field, 0, {"sub": near}).wait_recv()
        center(near_field, 1, {"sub": near}).wait_recv()
        pass_on(near_field, 0)

    def take_far_upper():
        center(far_field, 0, {"sub": far}).wait_recv()

        @pl.when(has_above)
        def _():
            upward(far_field).start()

    def take_far_lower():
        center(far_field, 1, {"sub": far}).wait_recv()

        @pl.when(has_below)
        def _():
            downward(far_field).start()
        pass_on(far_field, 0, True)

    def take_halo(f, stored=False):
        @pl.when(has_above)
        def _():
            downward(f).wait_recv()
            pass_on(f, 1, stored)

        @pl.when(has_below)
        def _():
            upward(f).wait_recv()
            pass_on(f, 2, stored)

    def settle(f):
        if n_lon > 1:
            sideways(f, 0).wait()

            @pl.when(has_above)
            def _():
                sideways(f, 1).wait()

            @pl.when(has_below)
            def _():
                sideways(f, 2).wait()

    def cast(f):
        for part in range(2):
            rows = pl.ds(part * HALO, HALO)
            sent[f, rows] = raw[f, rows].astype(BF16)

    for load in loads[:2]:
        load.wait()
    for load in loads[2:]:
        load.start()
    cast(near_field)
    pl.semaphore_wait(barrier, amount)

    @pl.when(has_far)
    def _():
        for part in range(2):
            center(near_field, part, {"sub": far}).start()
    cast(far_field)

    @pl.when(near_above)
    def _():
        direct(0).start()

    @pl.when(near_below)
    def _():
        direct(1).start()

    @pl.when(has_near)
    def _():
        for part in range(2):
            center(far_field, part, {"sub": near}).start()

    for load in loads[2:]:
        load.wait()
    count = count_ref[lat * n_lon + lon]
    tile = TILE
    chunks = slots // LANES
    place = (lax.broadcasted_iota(jnp.int32, (chunks, LANES), 0) * LANES
             + lax.broadcasted_iota(jnp.int32, (chunks, LANES), 1))
    slot_cols[...] = jnp.where(place < count, cols[...], -1)

    def adjoint_copy(t):
        rows = pl.ds(pl.multiple_of(t * tile, tile), tile)
        return pltpu.make_async_copy(adjoint.at[rows], adjoint_out.at[rows], adj_sem.at[t])

    def tangent_copy(t):
        rows = pl.ds(pl.multiple_of(t * tile, tile), tile)
        return pltpu.make_async_copy(tangent.at[rows], tangent_out.at[rows], tan_sem.at[t])

    def observe_columns(t):
        base = pl.multiple_of(t * tile, tile)
        rows = pl.ds(base, tile)
        wanted = lax.broadcasted_iota(jnp.int32, (tile, LANES), 0) + base
        hits = [jnp.where(slot_cols[k:k + 1, :] == wanted, 1.0, 0.0).astype(BF16) for k in range(chunks)]
        summed = dot(jnp.concatenate(hits, axis=1), cot[...]).astype(BF16)
        hidden = jnp.tanh(dot(back[rows, :], hw[...]) + bias[...])
        slopes = 1.0 - hidden * hidden
        state = sent[0, pl.ds(t * (tile // across), tile // across)].reshape(tile, levels)
        forward = dot(state, hw[...])
        per_column[rows, :] = dot((slopes * forward).astype(BF16), ow[...]).astype(BF16)
        pulled = dot_nt(summed, ow[...])
        adjoint[rows, :] = dot_nt((slopes * pulled).astype(BF16), hw[...])
        adjoint_copy(t).start()

    def observe_slots(t):
        parts = []
        for h in range(tile // LANES):
            named = jnp.transpose(jnp.broadcast_to(slot_cols[pl.ds(t * (tile // LANES) + h, 1), :], (LANES, LANES)))
            lane = lax.broadcasted_iota(jnp.int32, (LANES, LANES), 1)
            hits = [jnp.where(named == lane + c * LANES, 1.0, 0.0).astype(BF16) for c in range(columns // LANES)]
            parts.append(jnp.concatenate(hits, axis=1))
        tangent[pl.ds(pl.multiple_of(t * tile, tile), tile), :] = dot(
            jnp.concatenate(parts, axis=0), per_column[...]).astype(BF16)
        tangent_copy(t).start()

    def near_group(g):
        lanes = [pl.ds(pl.multiple_of(g * WIDE + h * LANES, LANES), LANES) for h in range(PAIR)]
        start, side_at = lon_places(lon, n_lon, across)
        transport_field(lat == 0, lat == n_lat - 1, start, side_at, field, side, near_field, lanes, rates,
                        near_field == 0, window, one, two, n_lon)
        for h in range(PAIR):
            moved[:, :, lanes[h]] = window[h, pl.ds(HALO, height), pl.ds(start, across), :]

    column_tiles, slot_tiles, groups = columns // tile, slots // tile, levels // WIDE
    pl.loop(0, column_tiles // 2)(observe_columns)

    @pl.when(has_near)
    def _():
        take_near_center()
    pl.loop(column_tiles // 2, column_tiles)(observe_columns)

    @pl.when(has_far)
    def _():
        take_far_upper()
    pl.loop(0, slot_tiles)(observe_slots)

    @pl.when(has_near)
    def _():
        take_halo(near_field)

    @pl.when(has_far)
    def _():
        take_far_lower()

    @pl.when(has_near)
    def _():
        settle(near_field)

    @pl.loop(0, groups)
    def _(g):
        @pl.when(jnp.logical_and(has_far, g == groups // 2))
        def _():
            take_halo(far_field, True)

        @pl.when(has_near)
        def _():
            near_group(g)

    kept = [pltpu.make_async_copy(moved, moved_out, moved_sem)]
    kept[0].start()

    @pl.when(has_near)
    def _():
        for part in range(2):
            center(far_field, part, {"sub": near}).wait_send()

    @pl.when(near_above)
    def _():
        direct(0).wait_send()

    @pl.when(near_below)
    def _():
        direct(1).wait_send()

    @pl.when(has_far)
    def _():
        settle(far_field)
        for part in range(2):
            center(near_field, part, {"sub": far}).wait_send()
        keep(far_field, 0).wait()

        @pl.when(has_above)
        def _():
            upward(far_field).wait_send()
            keep(far_field, 1).wait()

        @pl.when(has_below)
        def _():
            downward(far_field).wait_send()
            keep(far_field, 2).wait()

    if n_lon > 1:
        kept.append(pltpu.make_async_copy(side.at[far_field], side_out, load_sem.at[0]))
        kept[1].start()
    for item in kept:
        item.wait()
    for t in range(column_tiles):
        adjoint_copy(t).wait()
    for t in range(slot_tiles):
        tangent_copy(t).wait()


def exchange(sizes, count, cols, inc, mul, back, cot, hw, bias, ow, rates):
    height, across, levels = inc.shape
    columns = height * across
    slots, chan = cot.shape
    hid = hw.shape[1]
    total = height + 2 * HALO
    anywhere = pl.BlockSpec(memory_space=pl.ANY)
    vm = pltpu.VMEM
    dma = pltpu.SemaphoreType.DMA
    field_shape, side_shape = (2, total, across, levels), (2, total // 2, 2 * HALO, levels)
    flops = 2 * columns * levels * hid * 5 + 4 * columns * slots * chan
    window, state = transport_scratch(inc.shape, sizes[2])
    return pl.pallas_call(
        functools.partial(exchange_kernel, sizes),
        out_shape=(jax.ShapeDtypeStruct(field_shape[1:], BF16), jax.ShapeDtypeStruct(side_shape[1:], BF16),
                   jax.ShapeDtypeStruct((slots, chan), BF16), jax.ShapeDtypeStruct((columns, levels), F32), jax.ShapeDtypeStruct(inc.shape, F32)),
        in_specs=[pl.BlockSpec(memory_space=pltpu.SMEM)] + [anywhere] * 9,
        out_specs=(anywhere,) * 5,
        scratch_shapes=[
            vm(rates.shape, F32), vm(inc.shape, F32), window, state, state,
            vm(cols.shape, jnp.int32), vm((2,) + inc.shape, F32), vm((2,) + inc.shape, BF16),
            vm(back.shape, BF16), vm(cot.shape, BF16), vm(hw.shape, BF16), vm(bias.shape, F32), vm(ow.shape, BF16),
            vm(field_shape, BF16), vm(side_shape, BF16), vm(side_shape, BF16),
            vm((columns, chan), BF16), vm(cols.shape, jnp.int32), vm((slots, chan), BF16), vm((columns, levels), F32),
            dma((9,)), dma((2, KINDS)), dma((2, KINDS)), dma((3,)), dma((slots // TILE,)), dma((columns // TILE,)), dma,
        ],
        compiler_params=pltpu.CompilerParams(vmem_limit_bytes=VMEM_BYTES, collective_id=0, has_side_effects=True),
        cost_estimate=pl.CostEstimate(flops=flops, bytes_accessed=20 << 20, transcendentals=columns * hid),
        name="exchange",
    )(count, cols, inc, mul, back, cot, hw, bias, ow, rates)


def lon_places(lon, n_lon, across):
    if n_lon == 1:
        return 0, 0
    first = lon == 0
    return pl.multiple_of(jnp.where(first, 0, HALO), HALO), pl.multiple_of(jnp.where(first, across, 0), HALO)


def transport_scratch(shape, n_lon):
    height, across, _ = shape
    width = (across + (HALO if n_lon > 1 else 0)) // SUB
    total = height + 2 * HALO
    return (pltpu.VMEM((PAIR, total, width * SUB, LANES), F32),
            pltpu.VMEM((PAIR, total, width + 2 * REACH, SUB, LANES), F32))


def transport_field(lat_first, lat_last, start, side_at, field, side, f, lanes, rates, is_ahead, window, one, two, n_lon):
    total, width = window.shape[1], window.shape[2] // SUB
    across = field.shape[2]
    lane_row = lax.broadcasted_iota(jnp.int32, (SUB, LANES), 0)
    low_edge = lane_row == 0
    high_edge = lane_row == SUB - 1

    def put(ref, h, r, v, vec):
        ref[h, r, v + REACH] = vec
        if v >= width - REACH:
            ref[h, r, v - (width - REACH)] = jnp.where(low_edge, 0.0, pltpu.roll(vec, 1, 0))
        if v < REACH:
            ref[h, r, v + width + REACH] = jnp.where(high_edge, 0.0, pltpu.roll(vec, SUB - 1, 0))

    def clear_outside(ref):
        zero = jnp.zeros((PAIR, HALO) + ref.shape[2:], F32)

        @pl.when(lat_first)
        def _():
            ref[:, pl.ds(0, HALO)] = zero

        @pl.when(lat_last)
        def _():
            ref[:, pl.ds(total - HALO, HALO)] = zero

    def fill(h, p):
        if n_lon > 1:
            pair = side[f, p, :, lanes[h]].astype(F32)
        for q in range(2):
            window[h, 2 * p + q, pl.ds(start, across), :] = field[f, 2 * p + q, :, lanes[h]].astype(F32)
            if n_lon > 1:
                window[h, 2 * p + q, pl.ds(side_at, HALO), :] = pair[q * HALO:(q + 1) * HALO]

    @pl.loop(0, total // 2)
    def _(p):
        for h in range(PAIR):
            fill(h, p)

    @pl.loop(0, total // 2)
    def _(p):
        for h in range(PAIR):
            for q in range(2):
                for v in range(width):
                    put(one, h, 2 * p + q, v, window[h, 2 * p + q, pl.ds(v, SUB, stride=width), :])
    clear_outside(one)

    coeffs = []
    for h in range(PAIR):
        c = [jnp.where(is_ahead, rates[k:k + 1, lanes[h]], rates[m:m + 1, lanes[h]])
             for k, m in enumerate((3, 2, 1, 0, 7, 6, 5, 4))]
        rest = 1.0 - (((c[0] + c[1]) + (c[2] + c[3])) + ((c[4] + c[5]) + (c[6] + c[7])))
        scale = 1.0 / rest
        square = rest * rest
        coeffs.append([jnp.broadcast_to(x, (SUB, LANES)) for x in [x * scale for x in c] + [square * square]])

    def advance(src, dst, h, r, last):
        c = coeffs[h]
        lines = [[src[h, r + q, k] for k in range(2 * REACH)] for q in range(BLOCK)]
        for v in range(width):
            for q in range(BLOCK):
                lines[q].append(src[h, r + q, v + 2 * REACH])
            tall = ([src[h, r + k - REACH, v + REACH] for k in range(REACH)] + [line[v + REACH] for line in lines]
                    + [src[h, r + BLOCK + k, v + REACH] for k in range(REACH)])
            for q in range(BLOCK):
                line = lines[q][v:v + 2 * REACH + 1]
                acc = ((tall[q + 2] + c[0] * tall[q]) + (c[1] * tall[q + 1] + c[2] * tall[q + 3])
                       + (c[3] * tall[q + 4] + c[5] * line[1])
                       + ((c[4] * line[0] + c[6] * line[3]) + c[7] * line[4]))
                if last:
                    window[h, r + q, pl.ds(v, SUB, stride=width), :] = acc * c[8]
                else:
                    put(dst, h, r + q, v, acc)

    for step in range(STEPS):
        src, dst = (one, two) if step % 2 == 0 else (two, one)
        lo = REACH * (step + 1)

        @pl.loop(0, (total - 2 * lo) // BLOCK)
        def _(b):
            for h in range(PAIR):
                advance(src, dst, h, lo + b * BLOCK, step == STEPS - 1)
        if step < STEPS - 1:
            clear_outside(dst)


def transport_kernel(sizes, rates, field, side, moved, inc_ref, mul_ref, adj_ref, tangent, err_ref, grad_ref, tangent_out,
                     window, one, two):
    n_sub, n_lat, n_lon = sizes
    sub, lat, lon = lax.axis_index("sub"), lax.axis_index("lat"), lax.axis_index("lon")
    height, across = inc_ref.shape[0], inc_ref.shape[1]
    start, side_at = lon_places(lon, n_lon, across)
    odd = sub % 2
    far_is_ahead = odd == 0
    near = sub + 1 - 2 * odd
    far = sub - 1 + 2 * odd
    result = (pl.ds(HALO, height), pl.ds(start, across))
    lanes = [slice(h * LANES, (h + 1) * LANES) for h in range(PAIR)]
    tangent_out[...] = tangent[...]

    @pl.when(jnp.logical_and(far >= 0, far < n_sub))
    def _():
        transport_field(lat == 0, lat == n_lat - 1, start, side_at, field, side, 0, lanes, rates,
                        far_is_ahead, window, one, two, n_lon)

    @pl.when(jnp.logical_or(far < 0, far >= n_sub))
    def _():
        window[...] = jnp.zeros_like(window)
    for h in range(PAIR):
        part = (slice(None), slice(None), lanes[h])
        near_part = jnp.where(near < n_sub, moved[part], 0.0)
        far_part = window[(h,) + result]
        err_ref[part] = inc_ref[part] - jnp.where(far_is_ahead, far_part, near_part)
        grad_ref[part] = mul_ref[part] - jnp.where(far_is_ahead, near_part, far_part) + adj_ref[part]

def transport_call(sizes, rates, field, side, moved, inc, mul, adj, tangent):
    height, across, levels = inc.shape

    def whole(shape):
        return pl.BlockSpec(shape[:-1] + (WIDE,), lambda g: (0,) * (len(shape) - 1) + (g,))
    part = pl.BlockSpec((tangent.shape[0] * WIDE // levels, tangent.shape[1]), lambda g: (g, 0))
    arrays = (rates, field[None], side[None], moved, inc, mul, adj)
    window, state = transport_scratch(inc.shape, sizes[2])
    return pl.pallas_call(
        functools.partial(transport_kernel, sizes),
        grid=(levels // WIDE,),
        out_shape=(jax.ShapeDtypeStruct(inc.shape, F32),) * 2 + (jax.ShapeDtypeStruct(tangent.shape, BF16),),
        in_specs=[whole(x.shape) for x in arrays] + [part],
        out_specs=(whole(inc.shape),) * 2 + (part,),
        scratch_shapes=[window, state, state],
        compiler_params=pltpu.CompilerParams(vmem_limit_bytes=VMEM_BYTES),
        cost_estimate=pl.CostEstimate(flops=4 * 17 * height * across * levels, bytes_accessed=16 << 20, transcendentals=0),
        name="transport",
    )(*arrays, tangent)


def local(increment, multiplier, background, obs_cotangent, obs_column, obs_count, transport,
          hidden_weight, hidden_bias, output_weight):
    sizes = tuple(lax.axis_size(name) for name in ("sub", "lat", "lon"))
    assert sizes[2] <= 2
    inc, mul = increment[0], multiplier[0]
    levels = inc.shape[-1]
    field, side, tangent, adj, moved = exchange(
        sizes, obs_count[0], obs_column.reshape(-1, LANES), inc, mul, background.reshape(-1, levels),
        obs_cotangent[0, 0], hidden_weight, hidden_bias[None], output_weight, transport)
    err, grad, tangent = transport_call(sizes, transport, field, side, moved, inc, mul, adj.reshape(inc.shape), tangent)
    return err[None], grad[None], tangent[None, None]


def solution(mesh):
    field = P("sub", "lat", "lon", None)
    slots = P("sub", ("lat", "lon"), None, None)
    in_specs = (field, field, field, slots, P("sub", ("lat", "lon"), None), P("sub", None), P(), P(), P(), P())
    return jax.shard_map(local, mesh=mesh, in_specs=in_specs, out_specs=(field, field, slots), check_vma=False)
```

```python
import functools

import jax
import jax.numpy as jnp
from jax import lax
from jax.experimental import pallas as pl
from jax.experimental.pallas import tpu as pltpu
from jax.sharding import PartitionSpec as P

STEPS = 4
REACH = 2
HALO = STEPS * REACH
SUB = 8
LANES = 128
PAIR = 2
TILE = 512
WIDE = PAIR * LANES
BLOCK = 4
MESH = pl.DeviceIdType.MESH
NT = (((1,), (1,)), ((), ()))
F32 = jnp.float32
BF16 = jnp.bfloat16


def dot(a, b):
    return jnp.dot(a, b, preferred_element_type=F32)


def dot_nt(a, b):
    return lax.dot_general(a, b, NT, preferred_element_type=F32)


CENTER, UP, DOWN, SIDE = 0, 2, 3, 4
DIRECT = 7
KINDS = 9
VMEM_BYTES = 58 << 20


def exchange_kernel(sizes, count_ref, cols_hbm, inc_hbm, mul_hbm, back_hbm, cot_hbm, hw_hbm, bias_hbm, ow_hbm, rates_hbm,
                    field_out, side_out, tangent_out, adjoint_out, moved_out,
                    rates, moved, window, one, two, cols, raw, sent, back, cot, hw, bias, ow, field, side, stage,
                    per_column, slot_cols, tangent, adjoint,
                    load_sem, send_sem, recv_sem, out_sem, tan_sem, adj_sem, moved_sem):
    n_sub, n_lat, n_lon = sizes
    sub, lat, lon = lax.axis_index("sub"), lax.axis_index("lat"), lax.axis_index("lon")
    height, across, levels = inc_hbm.shape
    columns = height * across
    slots = cot.shape[0]
    odd = sub % 2
    near, far = sub + 1 - 2 * odd, sub - 1 + 2 * odd
    has_near = near < n_sub
    has_far = jnp.logical_and(far >= 0, far < n_sub)
    near_field, far_field = 1 - odd, odd
    has_above, has_below = lat > 0, lat < n_lat - 1

    loads = [(inc_hbm, raw.at[0]), (mul_hbm, raw.at[1]), (cols_hbm, cols), (cot_hbm, cot), (back_hbm, back),
             (hw_hbm, hw), (bias_hbm, bias), (ow_hbm, ow), (rates_hbm, rates)]
    loads = [pltpu.make_async_copy(a, b, load_sem.at[k]) for k, (a, b) in enumerate(loads)]
    for load in loads[:2]:
        load.start()

    barrier = pltpu.get_barrier_semaphore()
    near_above, near_below = jnp.logical_and(has_near, has_above), jnp.logical_and(has_near, has_below)
    others = [({"sub": near}, has_near), ({"sub": far}, has_far), ({"lat": lat - 1}, has_above), ({"lat": lat + 1}, has_below),
              ({"sub": near, "lat": lat - 1}, near_above), ({"sub": near, "lat": lat + 1}, near_below)]
    amount = sum(have.astype(jnp.int32) for _, have in others)
    for target, have in others:
        @pl.when(have)
        def _(target=target):
            pl.semaphore_signal(barrier, inc=1, device_id=target, device_id_type=MESH)
    if n_lon > 1:
        pl.semaphore_signal(barrier, inc=1, device_id={"lon": 1 - lon}, device_id_type=MESH)
        amount = amount + 1

    def copy(f, kind, src, dst, target):
        return pltpu.make_async_remote_copy(src_ref=src, dst_ref=dst, send_sem=send_sem.at[f, kind],
                                            recv_sem=recv_sem.at[f, kind], device_id=target, device_id_type=MESH)

    def center(f, part, target):
        return copy(f, CENTER + part, sent.at[f, pl.ds(part * HALO, HALO)],
                    field.at[f, pl.ds(HALO + part * HALO, HALO)], target)

    def upward(f):
        return copy(f, DOWN, field.at[f, pl.ds(HALO, HALO)], field.at[f, pl.ds(HALO + height, HALO)], {"lat": lat - 1})

    def downward(f):
        return copy(f, UP, field.at[f, pl.ds(height, HALO)], field.at[f, pl.ds(0, HALO)], {"lat": lat + 1})

    def direct(k):
        f, src, dst, row = ((far_field, 0, HALO + height, lat - 1), (far_field, height - HALO, 0, lat + 1))[k]
        return pltpu.make_async_remote_copy(
            src_ref=sent.at[f, pl.ds(src, HALO)], dst_ref=field.at[f, pl.ds(dst, HALO)],
            send_sem=send_sem.at[f, DIRECT + k], recv_sem=recv_sem.at[f, (DOWN, UP)[k]],
            device_id={"sub": near, "lat": row}, device_id_type=MESH)

    def sideways(f, k):
        lo, amount = ((HALO // 2, height // 2), (0, HALO // 2), ((HALO + height) // 2, HALO // 2))[k]
        return copy(f, SIDE + k, stage.at[f, pl.ds(lo, amount)], side.at[f, pl.ds(lo, amount)], {"lon": 1 - lon})

    def keep(f, k):
        lo, amount = ((HALO, height), (0, HALO), (HALO + height, HALO))[k]
        rows = pl.ds(lo, amount)
        return pltpu.make_async_copy(field.at[f, rows], field_out.at[rows], out_sem.at[k])

    def pass_on(f, k, stored=False):
        if stored:
            keep(f, k).start()
        if n_lon > 1:
            lo, amount = ((HALO // 2, height // 2), (0, HALO // 2), ((HALO + height) // 2, HALO // 2))[k]

            @pl.loop(lo, lo + amount)
            def _(p):
                pair = []
                for q in range(2):
                    row = field[f, 2 * p + q].astype(F32)
                    pair.append(jnp.where(lon == 0, row[across - HALO:], row[:HALO]))
                stage[f, p] = jnp.concatenate(pair, axis=0).astype(BF16)
            sideways(f, k).start()

    def take_near_center():
        center(near_field, 0, {"sub": near}).wait_recv()
        center(near_field, 1, {"sub": near}).wait_recv()
        pass_on(near_field, 0)

    def take_far_upper():
        center(far_field, 0, {"sub": far}).wait_recv()

        @pl.when(has_above)
        def _():
            upward(far_field).start()

    def take_far_lower():
        center(far_field, 1, {"sub": far}).wait_recv()

        @pl.when(has_below)
        def _():
            downward(far_field).start()
        pass_on(far_field, 0, True)

    def take_halo(f, stored=False):
        @pl.when(has_above)
        def _():
            downward(f).wait_recv()
            pass_on(f, 1, stored)

        @pl.when(has_below)
        def _():
            upward(f).wait_recv()
            pass_on(f, 2, stored)

    def settle(f):
        if n_lon > 1:
            sideways(f, 0).wait()

            @pl.when(has_above)
            def _():
                sideways(f, 1).wait()

            @pl.when(has_below)
            def _():
                sideways(f, 2).wait()

    def cast(f):
        for part in range(2):
            rows = pl.ds(part * HALO, HALO)
            sent[f, rows] = raw[f, rows].astype(BF16)

    for load in loads[:2]:
        load.wait()
    for load in loads[2:]:
        load.start()
    cast(near_field)
    pl.semaphore_wait(barrier, amount)

    @pl.when(has_far)
    def _():
        for part in range(2):
            center(near_field, part, {"sub": far}).start()
    cast(far_field)

    @pl.when(near_above)
    def _():
        direct(0).start()

    @pl.when(near_below)
    def _():
        direct(1).start()

    @pl.when(has_near)
    def _():
        for part in range(2):
            center(far_field, part, {"sub": near}).start()

    for load in loads[2:]:
        load.wait()
    count = count_ref[lat * n_lon + lon]
    tile = TILE
    chunks = slots // LANES
    place = (lax.broadcasted_iota(jnp.int32, (chunks, LANES), 0) * LANES
             + lax.broadcasted_iota(jnp.int32, (chunks, LANES), 1))
    slot_cols[...] = jnp.where(place < count, cols[...], -1)

    def adjoint_copy(t):
        rows = pl.ds(pl.multiple_of(t * tile, tile), tile)
        return pltpu.make_async_copy(adjoint.at[rows], adjoint_out.at[rows], adj_sem.at[t])

    def tangent_copy(t):
        rows = pl.ds(pl.multiple_of(t * tile, tile), tile)
        return pltpu.make_async_copy(tangent.at[rows], tangent_out.at[rows], tan_sem.at[t])

    def observe_columns(t):
        base = pl.multiple_of(t * tile, tile)
        rows = pl.ds(base, tile)
        wanted = lax.broadcasted_iota(jnp.int32, (tile, LANES), 0) + base
        hits = [jnp.where(slot_cols[k:k + 1, :] == wanted, 1.0, 0.0).astype(BF16) for k in range(chunks)]
        summed = dot(jnp.concatenate(hits, axis=1), cot[...]).astype(BF16)
        hidden = jnp.tanh(dot(back[rows, :], hw[...]) + bias[...])
        slopes = 1.0 - hidden * hidden
        state = sent[0, pl.ds(t * (tile // across), tile // across)].reshape(tile, levels)
        forward = dot(state, hw[...])
        per_column[rows, :] = dot((slopes * forward).astype(BF16), ow[...]).astype(BF16)
        pulled = dot_nt(summed, ow[...])
        adjoint[rows, :] = dot_nt((slopes * pulled).astype(BF16), hw[...])
        adjoint_copy(t).start()

    def observe_slots(t):
        parts = []
        for h in range(tile // LANES):
            named = jnp.transpose(jnp.broadcast_to(slot_cols[pl.ds(t * (tile // LANES) + h, 1), :], (LANES, LANES)))
            lane = lax.broadcasted_iota(jnp.int32, (LANES, LANES), 1)
            hits = [jnp.where(named == lane + c * LANES, 1.0, 0.0).astype(BF16) for c in range(columns // LANES)]
            parts.append(jnp.concatenate(hits, axis=1))
        tangent[pl.ds(pl.multiple_of(t * tile, tile), tile), :] = dot(
            jnp.concatenate(parts, axis=0), per_column[...]).astype(BF16)
        tangent_copy(t).start()

    def near_group(g):
        lanes = [pl.ds(pl.multiple_of(g * WIDE + h * LANES, LANES), LANES) for h in range(PAIR)]
        start, side_at = lon_places(lon, n_lon, across)
        transport_field(lat == 0, lat == n_lat - 1, start, side_at, field, side, near_field, lanes, rates,
                        near_field == 0, window, one, two, n_lon)
        for h in range(PAIR):
            moved[:, :, lanes[h]] = window[h, pl.ds(HALO, height), pl.ds(start, across), :]

    def moved_copy(g):
        lanes = pl.ds(pl.multiple_of(g * WIDE, WIDE), WIDE)
        return pltpu.make_async_copy(moved.at[:, :, lanes], moved_out.at[:, :, lanes], moved_sem.at[g])

    column_tiles, slot_tiles, groups = columns // tile, slots // tile, levels // WIDE
    pl.loop(0, column_tiles // 2)(observe_columns)

    @pl.when(has_near)
    def _():
        take_near_center()
    pl.loop(column_tiles // 2, column_tiles)(observe_columns)

    @pl.when(has_far)
    def _():
        take_far_upper()
    pl.loop(0, slot_tiles)(observe_slots)

    @pl.when(has_near)
    def _():
        take_halo(near_field)

    @pl.when(has_far)
    def _():
        take_far_lower()

    @pl.when(has_near)
    def _():
        settle(near_field)

    @pl.loop(0, groups)
    def _(g):
        @pl.when(jnp.logical_and(has_far, g == groups // 2))
        def _():
            take_halo(far_field, True)

        @pl.when(has_near)
        def _():
            near_group(g)
            moved_copy(g).start()

    kept = []

    @pl.when(has_near)
    def _():
        for g in range(groups):
            moved_copy(g).wait()
        for part in range(2):
            center(far_field, part, {"sub": near}).wait_send()

    @pl.when(near_above)
    def _():
        direct(0).wait_send()

    @pl.when(near_below)
    def _():
        direct(1).wait_send()

    @pl.when(has_far)
    def _():
        settle(far_field)
        for part in range(2):
            center(near_field, part, {"sub": far}).wait_send()
        keep(far_field, 0).wait()

        @pl.when(has_above)
        def _():
            upward(far_field).wait_send()
            keep(far_field, 1).wait()

        @pl.when(has_below)
        def _():
            downward(far_field).wait_send()
            keep(far_field, 2).wait()

    if n_lon > 1:
        kept.append(pltpu.make_async_copy(side.at[far_field], side_out, load_sem.at[0]))
        kept[0].start()
    for item in kept:
        item.wait()
    for t in range(column_tiles):
        adjoint_copy(t).wait()
    for t in range(slot_tiles):
        tangent_copy(t).wait()


def exchange(sizes, count, cols, inc, mul, back, cot, hw, bias, ow, rates):
    height, across, levels = inc.shape
    columns = height * across
    slots, chan = cot.shape
    hid = hw.shape[1]
    total = height + 2 * HALO
    anywhere = pl.BlockSpec(memory_space=pl.ANY)
    vm = pltpu.VMEM
    dma = pltpu.SemaphoreType.DMA
    field_shape, side_shape = (2, total, across, levels), (2, total // 2, 2 * HALO, levels)
    flops = 2 * columns * levels * hid * 5 + 4 * columns * slots * chan
    window, state = transport_scratch(inc.shape, sizes[2])
    return pl.pallas_call(
        functools.partial(exchange_kernel, sizes),
        out_shape=(jax.ShapeDtypeStruct(field_shape[1:], BF16), jax.ShapeDtypeStruct(side_shape[1:], BF16),
                   jax.ShapeDtypeStruct((slots, chan), BF16), jax.ShapeDtypeStruct((columns, levels), F32), jax.ShapeDtypeStruct(inc.shape, F32)),
        in_specs=[pl.BlockSpec(memory_space=pltpu.SMEM)] + [anywhere] * 9,
        out_specs=(anywhere,) * 5,
        scratch_shapes=[
            vm(rates.shape, F32), vm(inc.shape, F32), window, state, state,
            vm(cols.shape, jnp.int32), vm((2,) + inc.shape, F32), vm((2,) + inc.shape, BF16),
            vm(back.shape, BF16), vm(cot.shape, BF16), vm(hw.shape, BF16), vm(bias.shape, F32), vm(ow.shape, BF16),
            vm(field_shape, BF16), vm(side_shape, BF16), vm(side_shape, BF16),
            vm((columns, chan), BF16), vm(cols.shape, jnp.int32), vm((slots, chan), BF16), vm((columns, levels), F32),
            dma((9,)), dma((2, KINDS)), dma((2, KINDS)), dma((3,)), dma((slots // TILE,)), dma((columns // TILE,)), dma((levels // WIDE,)),
        ],
        compiler_params=pltpu.CompilerParams(vmem_limit_bytes=VMEM_BYTES, collective_id=0, has_side_effects=True),
        cost_estimate=pl.CostEstimate(flops=flops, bytes_accessed=20 << 20, transcendentals=columns * hid),
        name="exchange",
    )(count, cols, inc, mul, back, cot, hw, bias, ow, rates)


def lon_places(lon, n_lon, across):
    if n_lon == 1:
        return 0, 0
    first = lon == 0
    return pl.multiple_of(jnp.where(first, 0, HALO), HALO), pl.multiple_of(jnp.where(first, across, 0), HALO)


def transport_scratch(shape, n_lon):
    height, across, _ = shape
    width = (across + (HALO if n_lon > 1 else 0)) // SUB
    total = height + 2 * HALO
    return (pltpu.VMEM((PAIR, total, width * SUB, LANES), F32),
            pltpu.VMEM((PAIR, total, width + 2 * REACH, SUB, LANES), F32))


def transport_field(lat_first, lat_last, start, side_at, field, side, f, lanes, rates, is_ahead, window, one, two, n_lon):
    total, width = window.shape[1], window.shape[2] // SUB
    across = field.shape[2]
    lane_row = lax.broadcasted_iota(jnp.int32, (SUB, LANES), 0)
    low_edge = lane_row == 0
    high_edge = lane_row == SUB - 1

    def put(ref, h, r, v, vec):
        ref[h, r, v + REACH] = vec
        if v >= width - REACH:
            ref[h, r, v - (width - REACH)] = jnp.where(low_edge, 0.0, pltpu.roll(vec, 1, 0))
        if v < REACH:
            ref[h, r, v + width + REACH] = jnp.where(high_edge, 0.0, pltpu.roll(vec, SUB - 1, 0))

    def clear_outside(ref):
        zero = jnp.zeros((PAIR, HALO) + ref.shape[2:], F32)

        @pl.when(lat_first)
        def _():
            ref[:, pl.ds(0, HALO)] = zero

        @pl.when(lat_last)
        def _():
            ref[:, pl.ds(total - HALO, HALO)] = zero

    def fill(h, p):
        if n_lon > 1:
            pair = side[f, p, :, lanes[h]].astype(F32)
        for q in range(2):
            window[h, 2 * p + q, pl.ds(start, across), :] = field[f, 2 * p + q, :, lanes[h]].astype(F32)
            if n_lon > 1:
                window[h, 2 * p + q, pl.ds(side_at, HALO), :] = pair[q * HALO:(q + 1) * HALO]

    @pl.loop(0, total // 2)
    def _(p):
        for h in range(PAIR):
            fill(h, p)

    @pl.loop(0, total // 2)
    def _(p):
        for h in range(PAIR):
            for q in range(2):
                for v in range(width):
                    put(one, h, 2 * p + q, v, window[h, 2 * p + q, pl.ds(v, SUB, stride=width), :])
    clear_outside(one)

    coeffs = []
    for h in range(PAIR):
        c = [jnp.where(is_ahead, rates[k:k + 1, lanes[h]], rates[m:m + 1, lanes[h]])
             for k, m in enumerate((3, 2, 1, 0, 7, 6, 5, 4))]
        rest = 1.0 - (((c[0] + c[1]) + (c[2] + c[3])) + ((c[4] + c[5]) + (c[6] + c[7])))
        scale = 1.0 / rest
        square = rest * rest
        coeffs.append([jnp.broadcast_to(x, (SUB, LANES)) for x in [x * scale for x in c] + [square * square]])

    def advance(src, dst, h, r, last):
        c = coeffs[h]
        lines = [[src[h, r + q, k] for k in range(2 * REACH)] for q in range(BLOCK)]
        for v in range(width):
            for q in range(BLOCK):
                lines[q].append(src[h, r + q, v + 2 * REACH])
            tall = ([src[h, r + k - REACH, v + REACH] for k in range(REACH)] + [line[v + REACH] for line in lines]
                    + [src[h, r + BLOCK + k, v + REACH] for k in range(REACH)])
            for q in range(BLOCK):
                line = lines[q][v:v + 2 * REACH + 1]
                acc = ((tall[q + 2] + c[0] * tall[q]) + (c[1] * tall[q + 1] + c[2] * tall[q + 3])
                       + (c[3] * tall[q + 4] + c[5] * line[1])
                       + ((c[4] * line[0] + c[6] * line[3]) + c[7] * line[4]))
                if last:
                    window[h, r + q, pl.ds(v, SUB, stride=width), :] = acc * c[8]
                else:
                    put(dst, h, r + q, v, acc)

    for step in range(STEPS):
        src, dst = (one, two) if step % 2 == 0 else (two, one)
        lo = REACH * (step + 1)

        @pl.loop(0, (total - 2 * lo) // BLOCK)
        def _(b):
            for h in range(PAIR):
                advance(src, dst, h, lo + b * BLOCK, step == STEPS - 1)
        if step < STEPS - 1:
            clear_outside(dst)


def transport_kernel(sizes, rates_hbm, field_hbm, side_hbm, moved_hbm, inc_hbm, mul_hbm, adj_hbm, tangent_hbm,
                     err_hbm, grad_hbm, tangent_out,
                     rates, field, side, moved, inc, mul, adj, tangent, err, grad, window, one, two,
                     field_sem, load_sem, err_sem, grad_sem, tangent_sem):
    n_sub, n_lat, n_lon = sizes
    sub, lat, lon = lax.axis_index("sub"), lax.axis_index("lat"), lax.axis_index("lon")
    height, across, levels = inc.shape
    start, side_at = lon_places(lon, n_lon, across)
    odd = sub % 2
    far_is_ahead = odd == 0
    near = sub + 1 - 2 * odd
    far = sub - 1 + 2 * odd
    has_far = jnp.logical_and(far >= 0, far < n_sub)
    result = (pl.ds(HALO, height), pl.ds(start, across))
    groups = levels // WIDE

    def field_load(g):
        lanes = pl.ds(pl.multiple_of(g * WIDE, WIDE), WIDE)
        return pltpu.make_async_copy(field_hbm.at[:, :, :, lanes], field.at[:, :, :, lanes], field_sem.at[g])

    def store(src, dst, sem, g):
        lanes = pl.ds(pl.multiple_of(g * WIDE, WIDE), WIDE)
        return pltpu.make_async_copy(src.at[:, :, lanes], dst.at[:, :, lanes], sem.at[g])

    pairs = [(rates_hbm, rates), (side_hbm, side), (inc_hbm, inc), (moved_hbm, moved), (mul_hbm, mul), (adj_hbm, adj),
             (tangent_hbm, tangent)]
    loads = [pltpu.make_async_copy(x, y, load_sem.at[k]) for k, (x, y) in enumerate(pairs)]
    keep_tangent = pltpu.make_async_copy(tangent, tangent_out, tangent_sem)
    for load in loads[:2]:
        load.start()
    for g in range(groups):
        field_load(g).start()
    for load in loads[2:]:
        load.start()
    for load in loads[:2]:
        load.wait()

    @pl.loop(0, groups)
    def _(g):
        lanes = [pl.ds(pl.multiple_of(g * WIDE + h * LANES, LANES), LANES) for h in range(PAIR)]
        field_load(g).wait()

        @pl.when(has_far)
        def _():
            transport_field(lat == 0, lat == n_lat - 1, start, side_at, field, side, 0, lanes, rates,
                            far_is_ahead, window, one, two, n_lon)

        @pl.when(jnp.logical_not(has_far))
        def _():
            window[...] = jnp.zeros_like(window)

        @pl.when(g == 0)
        def _():
            for load in loads[2:]:
                load.wait()
            keep_tangent.start()
        for h in range(PAIR):
            part = (slice(None), slice(None), lanes[h])
            near_part = jnp.where(near < n_sub, moved[part], 0.0)
            far_part = window[(h,) + result]
            err[part] = inc[part] - jnp.where(far_is_ahead, far_part, near_part)
            grad[part] = mul[part] - jnp.where(far_is_ahead, near_part, far_part) + adj[part]
        store(err, err_hbm, err_sem, g).start()
        store(grad, grad_hbm, grad_sem, g).start()

    keep_tangent.wait()
    for g in range(groups):
        store(err, err_hbm, err_sem, g).wait()
        store(grad, grad_hbm, grad_sem, g).wait()


def transport_call(sizes, rates, field, side, moved, inc, mul, adj, tangent):
    height, across, levels = inc.shape
    anywhere = pl.BlockSpec(memory_space=pl.ANY)
    arrays = (rates, field[None], side[None], moved, inc, mul, adj, tangent)
    window, state = transport_scratch(inc.shape, sizes[2])
    dma = pltpu.SemaphoreType.DMA
    groups = levels // WIDE
    return pl.pallas_call(
        functools.partial(transport_kernel, sizes),
        out_shape=(jax.ShapeDtypeStruct(inc.shape, F32),) * 2 + (jax.ShapeDtypeStruct(tangent.shape, BF16),),
        in_specs=[anywhere] * len(arrays),
        out_specs=(anywhere,) * 3,
        scratch_shapes=[pltpu.VMEM(x.shape, x.dtype) for x in arrays + (inc, inc)] + [
            window, state, state, dma((groups,)), dma((7,)), dma((groups,)), dma((groups,)), dma],
        compiler_params=pltpu.CompilerParams(vmem_limit_bytes=VMEM_BYTES),
        cost_estimate=pl.CostEstimate(flops=4 * 17 * height * across * levels, bytes_accessed=18 << 20, transcendentals=0),
        name="transport",
    )(*arrays)


def local(increment, multiplier, background, obs_cotangent, obs_column, obs_count, transport,
          hidden_weight, hidden_bias, output_weight):
    sizes = tuple(lax.axis_size(name) for name in ("sub", "lat", "lon"))
    assert sizes[2] <= 2
    inc, mul = increment[0], multiplier[0]
    levels = inc.shape[-1]
    field, side, tangent, adj, moved = exchange(
        sizes, obs_count[0], obs_column.reshape(-1, LANES), inc, mul, background.reshape(-1, levels),
        obs_cotangent[0, 0], hidden_weight, hidden_bias[None], output_weight, transport)
    err, grad, tangent = transport_call(sizes, transport, field, side, moved, inc, mul, adj.reshape(inc.shape), tangent)
    return err[None], grad[None], tangent[None, None]


def solution(mesh):
    field = P("sub", "lat", "lon", None)
    slots = P("sub", ("lat", "lon"), None, None)
    in_specs = (field, field, field, slots, P("sub", ("lat", "lon"), None), P("sub", None), P(), P(), P(), P())
    return jax.shard_map(local, mesh=mesh, in_specs=in_specs, out_specs=(field, field, slots), check_vma=False)
```
